768 devices in a mesh: group: 64 (over x, y, core), dp: 12 (over z).
Axes of the slice: x: 4, y: 8, z: 12, core: 2. Of those that a mesh axis runs over, the one named last changes fastest.
Arguments:
- hidden: bfloat16 [64, 3072, 4096], P('group', 'dp'), may hold values from -6 to 6
- segment_ids: int32 [64, 12, 256], P('group', 'dp'), may hold values from 0 to 3, never falling along the last dimension, each value on 1 to 160 neighbouring positions
- assign: int32 [64, 48], P('group', 'dp'), may hold values from 0 to 47, each once within a row
- positive: int32 [64, 48], P(None, 'dp'), may hold values from 0 to 255, as said below
- gain: float32 [4096], replicated, may hold values from 0.1 to 1.9
Outputs:
- query_loss: float32 [64, 48], P('group', 'dp')
- grad_rows: bfloat16 [64, 3072, 4096], P('group', 'dp')
The draws below stay inside these ranges and needn't reach their ends.
Inputs may be any that keep to these rules, and one draw needn't show every extreme that they name: `segment_ids`: each passage is a run of rows of one device, every local passage has one row or more, and one passage per device has exactly 160 rows. Each row of assign is a permutation; value v names owner device v // 4 along dp and its slot v % 4. A passage's positive is never itself.
All inputs are finite; a program needn't handle non-finite values.
Results may differ from the reference program's by a relative error of at most 0.0067.
Values may be sent and summed in bfloat16 or wider, within the bound.
No kernel may reach another device: no remote copies, remote signals or barrier semaphores. Data moves between devices by JAX's collectives and lax.ppermute only.
A program may use at most 64 MiB of HBM per device.

```python
import math
import jax
import jax.numpy as jnp
import numpy as np
from jax import lax

D = 4096
ROWS = 256
PAS_DEV = 4
MOST = 160
BATCH = 256
OWNED = 48
N_GROUP = 64
N_DP = 12


def draw_positive(key, part):
    key = jax.random.fold_in(key, 7)
    column = jnp.arange(N_DP * PAS_DEV) % PAS_DEV
    selfpos = jnp.arange(N_GROUP)[:, None] * PAS_DEV + column[None, :]
    offset = jax.random.randint(key, (N_GROUP, N_DP * PAS_DEV), 1, BATCH)
    return ((selfpos + offset) % BATCH).astype(jnp.int32)


def levels(stream_key, extent, cuts, smallest, largest):
    level = 1.0
    for axis_at, shards_of in cuts:
        heights = jax.random.uniform(jax.random.fold_in(jax.random.fold_in(stream_key, 6), axis_at), (shards_of,), jnp.float32, smallest / len(cuts), largest / len(cuts))
        level = level * jnp.repeat(jnp.exp(heights), extent[axis_at] // shards_of).reshape((-1,) + (1,) * (len(extent) - 1 - axis_at))
    return level


def split_up(count, total, bound, skew):
    portions = [(1 << 20) // math.isqrt(standing ** skew) + 1 for standing in range(2, count + 1)]
    surplus, given = total - bound - (count - 1), [1] * (count - 1)
    while surplus > 0:
        candidates = [i for i in range(count - 1) if given[i] < bound]
        mass, budget = sum([portions[i] for i in candidates]), surplus
        for i in candidates:
            more = min(bound - given[i], max(1, budget * portions[i] // mass), surplus)
            given[i] = given[i] + more
            surplus = surplus - more
    return np.array([bound] + given)


def uneven(stream_key, count, total, most, skew):
    if count == 2:
        one = jax.random.randint(stream_key, (), max(1, total - most), min(most, total - 1) + 1)
        return jnp.stack([one, total - one])
    lengths = jnp.asarray(split_up(count, total, most, skew), jnp.int32)
    pairs = (count - 1) // 2
    donor, taker = lengths[1:1 + 2 * pairs:2], lengths[2:2 + 2 * pairs:2]
    margin = jnp.minimum(donor - 1, most - taker)
    shifted = jax.random.randint(jax.random.fold_in(stream_key, 1), (pairs,), 0, 1 << 20) % (margin + 1)
    lengths = lengths.at[1:1 + 2 * pairs:2].set(donor - shifted).at[2:2 + 2 * pairs:2].set(taker + shifted)
    return lengths[jax.random.permutation(jax.random.fold_in(stream_key, 2), count)]


def noise(rng, extent, deviation, most, pieces=(), dtype=jnp.bfloat16):
    values = deviation * jax.random.normal(rng, extent, jnp.float32)
    if pieces:
        values = values * levels(rng, extent, pieces, -0.22, 0.18)
    return jnp.clip(values, -most, most).astype(dtype)


def setup_inputs(seed: int = 0) -> dict:
    seeds = jax.random.split(jax.random.key(seed), 6)
    return {
        "hidden": noise(seeds[0], (N_GROUP, N_DP * ROWS, D), 1.0, 6.0, ((0, 64), (1, 12))),
        "segment_ids": jax.vmap(lambda own: jnp.searchsorted(jnp.cumsum(uneven(own, PAS_DEV, ROWS, MOST, 2)), jnp.arange(ROWS), side="right"))(jax.random.split(seeds[1], N_GROUP * N_DP)).reshape((N_GROUP, N_DP, ROWS)).astype(jnp.int32),
        "assign": jax.vmap(lambda own: jax.random.permutation(own, OWNED))(jax.random.split(seeds[2], N_GROUP)).reshape((N_GROUP, OWNED)).astype(jnp.int32),
        "positive": draw_positive(jax.random.fold_in(seeds[5], 71), 0),
        "gain": jnp.clip(1.0 + 0.18 * jax.random.normal(seeds[4], (D,), jnp.float32), 0.1, 1.9),
    }


inv_tau = 20.0
loss_scale = 1024.0
norm_eps = 1e-06

def row_stats(rows_in, gain):
    values = rows_in.astype(jnp.float32)
    inverse = lax.rsqrt(lax.optimization_barrier(jnp.mean(values * values, axis=-1, keepdims=True)) + norm_eps)
    return (values, inverse)

def pool_block(rows_in, segment_row, gain):
    values, inverse = row_stats(rows_in, gain)
    normed = values * inverse * gain
    onehot = (segment_row[None, :] == jnp.arange(PAS_DEV)[:, None]).astype(jnp.float32)
    counts = lax.optimization_barrier(jnp.sum(onehot, axis=1))
    pooled = jnp.dot(onehot, normed, precision=lax.Precision.HIGHEST, preferred_element_type=jnp.float32)
    return (pooled / counts[:, None]).astype(jnp.bfloat16)

def contrast(embeds, positives):
    values = embeds.astype(jnp.float32)
    length = jnp.sqrt(lax.optimization_barrier(jnp.sum(values * values, axis=-1, keepdims=True)) + norm_eps)
    unit = values / length
    unit_bf = unit.astype(jnp.bfloat16)
    logits = jnp.dot(unit_bf, unit_bf.T, preferred_element_type=jnp.float32) * inv_tau
    index = jnp.arange(BATCH)
    logits = jnp.where(index[:, None] == index[None, :], -1e+30, logits)
    top = lax.optimization_barrier(jnp.max(logits, axis=-1, keepdims=True))
    lse = top[:, 0] + jnp.log(lax.optimization_barrier(jnp.sum(jnp.exp(logits - top), axis=-1)))
    hits = index[None, :] == positives[:, None]
    target = lax.optimization_barrier(jnp.sum(jnp.where(hits, logits, 0.0), axis=-1))
    loss = lse - target
    prob = jnp.exp(logits - lse[:, None])
    weights = (loss_scale * (prob - hits.astype(jnp.float32))).astype(jnp.bfloat16)
    grad_unit = jnp.dot(weights, unit_bf, preferred_element_type=jnp.float32) * inv_tau
    grad_unit = grad_unit + jnp.dot(weights.T, unit_bf, preferred_element_type=jnp.float32) * inv_tau
    inner = lax.optimization_barrier(jnp.sum(unit * grad_unit, axis=-1, keepdims=True))
    grad_embed = ((grad_unit - unit * inner) / length).astype(jnp.bfloat16)
    return (loss, grad_embed)

def row_backward(rows_in, segment_row, grad_embed, gain):
    values, inverse = row_stats(rows_in, gain)
    onehot = (segment_row[None, :] == jnp.arange(PAS_DEV)[:, None]).astype(jnp.float32)
    counts = lax.optimization_barrier(jnp.sum(onehot, axis=1))
    scaled = grad_embed.astype(jnp.float32) / counts[:, None]
    spread = jnp.dot(onehot.T, scaled, precision=lax.Precision.HIGHEST, preferred_element_type=jnp.float32)
    gained = gain * spread
    grad = inverse * gained - values * inverse ** 3 * lax.optimization_barrier(jnp.mean(values * gained, axis=-1, keepdims=True))
    return grad.astype(jnp.bfloat16)

def reference(hidden, segment_ids, assign, positive, gain):
    blocks = hidden.reshape(N_GROUP * N_DP, ROWS, D)
    segs = segment_ids.reshape(N_GROUP * N_DP, ROWS)
    pooled = lax.map(lambda pair: pool_block(pair[0], pair[1], gain), (blocks, segs))
    pooled = pooled.reshape(N_GROUP, OWNED, D)
    owned = jax.vmap(lambda emb, where: jnp.zeros_like(emb).at[where].set(emb))(pooled, assign)
    batches = owned.reshape(N_GROUP, N_DP, PAS_DEV, D).transpose(1, 0, 2, 3).reshape(N_DP, BATCH, D)
    partners = positive.reshape(N_GROUP, N_DP, PAS_DEV).transpose(1, 0, 2).reshape(N_DP, BATCH)
    losses, grads = lax.map(lambda pair: contrast(pair[0], pair[1]), (batches, partners))
    query_loss = losses.reshape(N_DP, N_GROUP, PAS_DEV).transpose(1, 0, 2).reshape(N_GROUP, OWNED)
    grad_owned = grads.reshape(N_DP, N_GROUP, PAS_DEV, D).transpose(1, 0, 2, 3).reshape(N_GROUP, OWNED, D)
    grad_local = jax.vmap(lambda gvals, where: gvals[where])(grad_owned, assign)
    grad_local = grad_local.reshape(N_GROUP * N_DP, PAS_DEV, D)
    grad_rows = lax.map(lambda trio: row_backward(trio[0], trio[1], trio[2], gain), (blocks, segs, grad_local))
    return (query_loss, grad_rows.reshape(N_GROUP, N_DP * ROWS, D))
```

```python
import functools

import jax
import jax.numpy as jnp
from jax import lax
from jax.experimental import pallas as pl
from jax.experimental.pallas import tpu as pltpu
from jax.sharding import Mesh
from jax.sharding import PartitionSpec as P

inv_tau = 20.0
loss_scale = 1024.0
norm_eps = 1e-06

F32 = jnp.float32
BF16 = jnp.bfloat16
ROWS = 256
D = 4096
HALF = D // 2
PAS = 4
META = 128
N_DP = 12
N_XY = 32
BATCH = 256

VMEM = pl.BlockSpec(memory_space=pltpu.VMEM)
SMEM = pl.BlockSpec(memory_space=pltpu.SMEM)
PARAMS = pltpu.CompilerParams(vmem_limit_bytes=40 * 1024 * 1024)


def iota(shape, dim):
    return lax.broadcasted_iota(jnp.int32, shape, dim)


def split3(values):
    high = values.astype(BF16).astype(F32)
    rest = values - high
    middle = rest.astype(BF16).astype(F32)
    low = rest - middle
    return jnp.concatenate([high, middle, low], axis=0).astype(BF16)


def sum3(values):
    return values[0:8] + values[8:16] + values[16:24]


def pool_kernel(hidden_ref, segment_ref, assign_ref, gain_ref, send_ref, inverse_ref, squares):
    def block(at, carry):
        rows = pl.ds(pl.multiple_of(at * 16, 16), 16)
        values = hidden_ref[0, rows, :].astype(F32)
        total = jnp.sum(values * values, axis=1, keepdims=True)
        squares[rows, :] = jnp.broadcast_to(total, (16, 128))
        return carry

    lax.fori_loop(0, ROWS // 16, block, 0)
    inverse = lax.rsqrt(squares[...].T[0:8] * (1.0 / D) + norm_eps)
    inverse_ref[...] = inverse
    segment = jnp.broadcast_to(segment_ref[0], (8, ROWS))
    onehot = jnp.where(segment == iota((8, ROWS), 0), 1.0, 0.0)
    counts = jnp.maximum(jnp.sum(onehot, axis=1, keepdims=True), 1.0)
    weights = split3(onehot * inverse)
    slot = iota((8, META), 0)
    meta = jnp.zeros((8, META), F32)
    for k in range(PAS):
        meta = jnp.where(lax.rem(slot, PAS) == k, assign_ref[0, k].astype(F32), meta)
    lane = lax.axis_index("dp") * 8 + slot
    meta = jnp.where(iota((8, META), 1) == lane, meta, 0.0).astype(BF16)
    halves = []
    for h in range(2):
        columns = pl.ds(h * HALF, HALF)
        pooled = sum3(jnp.dot(weights, hidden_ref[0, :, columns], preferred_element_type=F32))
        halves.append((pooled * gain_ref[:, columns] / counts)[0:PAS])
    packed = jnp.concatenate(halves, axis=0).astype(BF16)
    for peer in range(N_DP):
        send_ref[peer, :, 0:HALF] = packed
        send_ref[peer, :, HALF:] = meta


def unit_kernel(pooled_ref, send_ref, embed_ref, length_ref):
    core = lax.axis_index("core")
    wanted = lax.axis_index("dp") * PAS
    row = iota((8, META), 0)
    lane = iota((8, META), 1)
    embeds, lengths = [], []
    for c in range(2):
        owners = jnp.sum(pooled_ref[c, :, HALF:].astype(F32), axis=0, keepdims=True)
        hit = (owners == (wanted + lax.rem(row, PAS)).astype(F32)) & (
            lax.div(lax.rem(lane, 8), PAS) == lax.div(row, PAS)
        )
        select = jnp.where(hit & (lane < N_DP * 8), 1.0, 0.0)[:, : N_DP * 8].astype(BF16)
        embed = jnp.dot(select, pooled_ref[c, :, 0:HALF], preferred_element_type=F32)
        squares = jnp.sum(embed * embed, axis=1, keepdims=True)
        squares = squares[0:PAS] + squares[PAS:]
        embeds.append(embed)
        lengths.append(jnp.sqrt(squares + norm_eps))
    length = jnp.concatenate(lengths, axis=0)
    own = jnp.where(
        core == 0,
        jnp.concatenate([embeds[0][0:PAS], embeds[1][0:PAS]], axis=0),
        jnp.concatenate([embeds[0][PAS:], embeds[1][PAS:]], axis=0),
    )
    embed_ref[...] = own
    length_ref[...] = jnp.broadcast_to(length, (8, 128))
    unit = (own / length).astype(BF16)
    for peer in range(N_XY):
        send_ref[peer] = unit


def gram_kernel(unit_ref, embed_ref, gram_ref):
    units = unit_ref[...]
    dims = (((1,), (1,)), ((), ()))
    gram_ref[0:BATCH] = lax.dot_general(units, units, dims, preferred_element_type=F32)
    gram_ref[BATCH:] = lax.dot_general(
        embed_ref[...].astype(BF16), units, dims, preferred_element_type=F32
    )


def contrast_kernel(gram_ref, unit_ref, embed_ref, length_ref, positive_ref, loss_ref, send_ref):
    core = lax.axis_index("core")
    first = (lax.axis_index("x") * 8 + lax.axis_index("y")) * 8
    shift = inv_tau
    row = iota((8, BATCH), 0)
    lane = iota((8, BATCH), 1)
    mine = first + row
    lanes = iota((64, BATCH), 1)
    partner = jnp.zeros((64, BATCH), jnp.int32)
    for s in range(PAS):
        partner = jnp.where(lax.rem(lanes, PAS) == s, positive_ref[:, s : s + 1], partner)
    partner = jnp.where(lax.div(lanes, PAS) == iota((64, BATCH), 0), partner, 0)
    partner = jnp.sum(partner, axis=0, keepdims=True)
    own_partner = jnp.sum(jnp.where(lane == mine, partner, 0), axis=1, keepdims=True)

    logits = (gram_ref[0, 0:BATCH] + gram_ref[1, 0:BATCH]) * inv_tau
    everyone = iota((BATCH, BATCH), 0) == iota((BATCH, BATCH), 1)
    logits = jnp.where(everyone, -1e30, logits)
    lse_all = shift + jnp.log(jnp.sum(jnp.exp(logits - shift), axis=0, keepdims=True))
    at = pl.ds(pl.multiple_of(first, 8), 8)
    own = (gram_ref[0, at, :] + gram_ref[1, at, :]) * inv_tau
    own = jnp.where(lane == mine, -1e30, own)
    lse = shift + jnp.log(jnp.sum(jnp.exp(own - shift), axis=1, keepdims=True))
    hits = lane == own_partner
    loss = lse - jnp.sum(jnp.where(hits, own, 0.0), axis=1, keepdims=True)
    as_query = loss_scale * (jnp.exp(own - lse) - jnp.where(hits, 1.0, 0.0))
    as_key = loss_scale * (jnp.exp(own - lse_all) - jnp.where(partner == mine, 1.0, 0.0))
    weights = jnp.concatenate([as_query, as_key], axis=0).astype(BF16)
    grad = jnp.dot(weights, unit_ref[...], preferred_element_type=F32)
    grad = (grad[0:8] + grad[8:16]) * inv_tau
    weights = weights.astype(F32)
    length = length_ref[:, 0:1]
    along = (gram_ref[0, BATCH:] + gram_ref[1, BATCH:]) / length
    inner = inv_tau * jnp.sum((weights[0:8] + weights[8:16]) * along, axis=1, keepdims=True)
    grad = ((grad - embed_ref[...] / length * inner) / length).astype(BF16)
    for peer in range(N_DP):
        send_ref[peer] = grad
    place = (iota((8, 128), 1) + core * PAS) == iota((8, 128), 0)
    loss = jnp.sum(jnp.where(place, loss, 0.0), axis=0, keepdims=True)
    loss_ref[...] = loss[:, 0:PAS]


def rows_kernel(
    grad_ref, hidden_ref, segment_ref, assign_ref, gain_ref, inverse_ref, out_ref, scaled, coef
):
    core = lax.axis_index("core")
    row = iota((8, N_DP * 8), 0)
    lane = iota((8, N_DP * 8), 1)
    select = jnp.zeros((8, N_DP * 8), F32)
    for k in range(PAS):
        owner = assign_ref[0, k]
        at = lax.div(owner, PAS) * 8 + core * PAS + lax.rem(owner, PAS)
        select = jnp.where((row == k) & (lane == at), 1.0, select)
    select = select.astype(BF16)
    segment = jnp.broadcast_to(segment_ref[0], (8, ROWS))
    onehot = jnp.where(segment == iota((8, ROWS), 0), 1.0, 0.0)
    counts = jnp.maximum(jnp.sum(onehot, axis=1, keepdims=True), 1.0)
    for h in range(2):
        columns = pl.ds(h * HALF, HALF)
        part = jnp.dot(select, grad_ref[h], preferred_element_type=F32)
        scaled[:, columns] = split3(gain_ref[:, columns] * (part / counts))
    upright = jnp.concatenate(
        [onehot, onehot, onehot, inverse_ref[...], jnp.zeros((96, ROWS), F32)], axis=0
    ).T
    spread = upright[:, 0:24]
    inverse = upright[:, 24:25]
    dots = lax.dot_general(
        hidden_ref[0], scaled[...], (((1,), (1,)), ((), ())), preferred_element_type=F32
    )
    dot = jnp.sum(dots * spread, axis=1, keepdims=True) * (1.0 / D)
    coef[:, 0:128] = jnp.broadcast_to(inverse, (ROWS, 128))
    coef[:, 128:256] = jnp.broadcast_to(inverse * inverse * inverse * dot, (ROWS, 128))
    spread = spread.astype(BF16)
    width = 512
    for at in range(0, D, width):
        columns = pl.ds(at, width)
        gained = jnp.dot(spread, scaled[:, columns], preferred_element_type=F32)
        values = hidden_ref[0, :, columns].astype(F32)
        out_ref[0, :, columns] = (
            coef[:, 0:1] * gained - values * coef[:, 128:129]
        ).astype(BF16)


def local(hidden, segment_ids, assign, positive, gain):
    shape = jax.ShapeDtypeStruct
    gain = gain.reshape(1, D)
    with jax.named_scope("pool"):
        send, inverse = pl.pallas_call(
            pool_kernel,
            out_shape=(shape((N_DP, 8, HALF + META), BF16), shape((8, ROWS), F32)),
            in_specs=[VMEM, VMEM, SMEM, VMEM],
            out_specs=(VMEM, VMEM),
            scratch_shapes=[pltpu.VMEM((ROWS, 128), F32)],
            compiler_params=PARAMS,
        )(hidden, segment_ids, assign, gain)
    with jax.named_scope("pooled_exchange"):
        pooled = lax.all_to_all(send, "dp", 0, 0)
        pooled = lax.all_gather(pooled.reshape(N_DP * 8, HALF + META), "core", axis=0)
    with jax.named_scope("unit"):
        send, embed, length = pl.pallas_call(
            unit_kernel,
            out_shape=(shape((N_XY, 8, HALF), BF16), shape((8, HALF), F32), shape((8, 128), F32)),
            in_specs=[VMEM],
            out_specs=(VMEM, VMEM, VMEM),
            compiler_params=PARAMS,
        )(pooled)
    with jax.named_scope("unit_exchange"):
        units = lax.all_to_all(send, ("x", "y"), 0, 0).reshape(BATCH, HALF)
    with jax.named_scope("gram"):
        gram = pl.pallas_call(
            gram_kernel,
            out_shape=shape((BATCH + 8, BATCH), F32),
            in_specs=[VMEM, VMEM],
            out_specs=VMEM,
            compiler_params=PARAMS,
        )(units, embed)
        gram = lax.all_gather(gram, "core", axis=0)
    with jax.named_scope("contrast"):
        loss, send = pl.pallas_call(
            contrast_kernel,
            out_shape=(shape((1, PAS), F32), shape((N_DP, 8, HALF), BF16)),
            in_specs=[VMEM] * 5,
            out_specs=(VMEM, VMEM),
            compiler_params=PARAMS,
        )(gram, units, embed, length, positive)
    with jax.named_scope("grad_exchange"):
        grads = lax.all_to_all(send, "dp", 0, 0)
        grads = lax.all_gather(grads.reshape(N_DP * 8, HALF), "core", axis=0)
    with jax.named_scope("rows"):
        grad_rows = pl.pallas_call(
            rows_kernel,
            out_shape=shape((1, ROWS, D), BF16),
            in_specs=[VMEM, VMEM, VMEM, SMEM, VMEM, VMEM],
            out_specs=VMEM,
            scratch_shapes=[pltpu.VMEM((24, D), BF16), pltpu.VMEM((ROWS, 256), F32)],
            compiler_params=PARAMS,
        )(grads, hidden, segment_ids, assign, gain, inverse)
    return loss, grad_rows


def solution(mesh):
    fine = Mesh(mesh.devices.reshape(4, 8, 2, N_DP), ("x", "y", "core", "dp"))
    group = ("x", "y", "core")
    placed = (P(group, "dp", None), P(group, "dp", None), P(group, "dp"), P(None, "dp"), P())
    return jax.shard_map(
        local,
        mesh=fine,
        in_specs=placed,
        out_specs=(P(group, "dp"), P(group, "dp", None)),
        check_vma=False,
    )
```

```python
import functools

import jax
import jax.numpy as jnp
from jax import lax
from jax.experimental import pallas as pl
from jax.experimental.pallas import tpu as pltpu
from jax.sharding import Mesh
from jax.sharding import PartitionSpec as P

inv_tau = 20.0
loss_scale = 1024.0
norm_eps = 1e-06

F32 = jnp.float32
BF16 = jnp.bfloat16
ROWS = 256
D = 4096
HALF = D // 2
PAS = 4
CHUNK = 64
N_DP = 12
N_XY = 32
BATCH = 256

VMEM = pl.BlockSpec(memory_space=pltpu.VMEM)
SMEM = pl.BlockSpec(memory_space=pltpu.SMEM)
HBM = pl.BlockSpec(memory_space=pltpu.HBM)
PARAMS = pltpu.CompilerParams(vmem_limit_bytes=40 * 1024 * 1024)


def iota(shape, dim):
    return lax.broadcasted_iota(jnp.int32, shape, dim)


def split3(values):
    high = values.astype(BF16).astype(F32)
    rest = values - high
    middle = rest.astype(BF16).astype(F32)
    low = rest - middle
    return jnp.concatenate([high, middle, low], axis=0).astype(BF16)


def sum3(values):
    return values[0:8] + values[8:16] + values[16:24]


def pool_kernel(
    hidden_hbm, segment_hbm, assign_hbm, gain_hbm, positive_hbm,
    send_ref, upright_ref, partner_ref,
    hidden, segment_at, assign_at, gain, positive, squares, chunk_sem, small_sem,
):
    chunks = [pl.ds(at * CHUNK, CHUNK) for at in range(ROWS // CHUNK)]
    copies = [
        pltpu.make_async_copy(hidden_hbm.at[0, rows], hidden.at[rows], chunk_sem.at[at])
        for at, rows in enumerate(chunks)
    ]
    small = [
        pltpu.make_async_copy(source, target, small_sem.at[at])
        for at, (source, target) in enumerate(
            [(segment_hbm, segment_at), (assign_hbm, assign_at), (positive_hbm, positive), (gain_hbm, gain)]
        )
    ]
    copies[0].start()
    for copy in small:
        copy.start()
    for copy in copies[1:]:
        copy.start()

    for copy in small:
        copy.wait()
    segment = jnp.broadcast_to(segment_at[0], (8, ROWS))
    onehot = jnp.where(segment == iota((8, ROWS), 0), 1.0, 0.0)
    counts = jnp.maximum(jnp.sum(onehot, axis=1, keepdims=True), 1.0)
    row = iota((N_DP * 8, 8), 0)
    lane = iota((N_DP * 8, 8), 1)
    owner = jnp.zeros((N_DP * 8, 8), jnp.int32)
    for k in range(PAS):
        owner = jnp.where(lax.rem(lane, PAS) == k, assign_at[0:1, k : k + 1], owner)
    slot = lax.div(row, 8) * PAS + lax.rem(row, PAS)
    place = (owner == slot) & (lax.div(lax.rem(row, 8), PAS) == lax.div(lane, PAS))
    place = jnp.where(place, 1.0, 0.0).astype(BF16)
    lane = iota((64, BATCH), 1)
    spread = jnp.where(lax.div(lane, PAS) == iota((64, BATCH), 0), 1.0, 0.0).astype(BF16)
    partner = jnp.concatenate([positive[...].astype(F32), jnp.zeros((PAS, 64), F32)], axis=0)
    partner = jnp.dot(partner.astype(BF16), spread, preferred_element_type=F32)
    partner = jnp.where(lax.rem(iota((8, BATCH), 1), PAS) == iota((8, BATCH), 0), partner, 0.0)
    partner_ref[...] = jnp.sum(partner, axis=0, keepdims=True).astype(jnp.int32)

    for at in range(ROWS // CHUNK):
        copies[at].wait()

        def block(step, carry):
            rows = pl.ds(pl.multiple_of(at * CHUNK + step * 16, 16), 16)
            values = hidden[rows, :].astype(F32)
            total = jnp.sum(values * values, axis=1, keepdims=True)
            squares[rows, :] = jnp.broadcast_to(total, (16, 128))
            return carry

        lax.fori_loop(0, CHUNK // 16, block, 0)
    inverse = lax.rsqrt(squares[...].T[0:8] * (1.0 / D) + norm_eps)
    weights = split3(onehot * inverse)
    halves = []
    for h in range(2):
        columns = pl.ds(h * HALF, HALF)
        pooled = sum3(jnp.dot(weights, hidden[:, columns], preferred_element_type=F32))
        halves.append((pooled * gain[:, columns] / counts)[0:PAS])
    packed = jnp.concatenate(halves, axis=0).astype(BF16)
    placed = jnp.dot(place, packed, preferred_element_type=F32).astype(BF16)
    send_ref[...] = placed.reshape(N_DP, 8, HALF)
    upright_ref[...] = jnp.concatenate(
        [onehot, onehot, onehot, inverse, jnp.zeros((96, ROWS), F32)], axis=0
    ).T


def unit_kernel(pooled_ref, send_ref, embed_ref, length_ref):
    core = lax.axis_index("core")
    embeds, lengths = [], []
    for c in range(2):
        embed = pooled_ref[c, 0].astype(F32)
        for peer in range(1, N_DP):
            embed = embed + pooled_ref[c, peer].astype(F32)
        squares = jnp.sum(embed * embed, axis=1, keepdims=True)
        squares = squares[0:PAS] + squares[PAS:]
        embeds.append(embed)
        lengths.append(jnp.sqrt(squares + norm_eps))
    length = jnp.concatenate(lengths, axis=0)
    own = jnp.where(
        core == 0,
        jnp.concatenate([embeds[0][0:PAS], embeds[1][0:PAS]], axis=0),
        jnp.concatenate([embeds[0][PAS:], embeds[1][PAS:]], axis=0),
    )
    embed_ref[...] = own
    length_ref[...] = jnp.broadcast_to(length, (8, 128))
    unit = (own / length).astype(BF16)
    for peer in range(N_XY):
        send_ref[peer] = unit


def gram_kernel(unit_ref, embed_ref, gram_ref):
    units = unit_ref[...]
    dims = (((1,), (1,)), ((), ()))
    gram_ref[0:BATCH] = lax.dot_general(units, units, dims, preferred_element_type=F32)
    gram_ref[BATCH:] = lax.dot_general(
        embed_ref[...].astype(BF16), units, dims, preferred_element_type=F32
    )


def contrast_kernel(gram_ref, unit_ref, embed_ref, length_ref, partner_ref, loss_ref, send_ref):
    core = lax.axis_index("core")
    first = (lax.axis_index("x") * 8 + lax.axis_index("y")) * 8
    shift = inv_tau
    row = iota((8, BATCH), 0)
    lane = iota((8, BATCH), 1)
    mine = first + row
    partner = partner_ref[...]
    own_partner = jnp.sum(jnp.where(lane == mine, partner, 0), axis=1, keepdims=True)

    logits = (gram_ref[0, 0:BATCH] + gram_ref[1, 0:BATCH]) * inv_tau
    everyone = iota((BATCH, BATCH), 0) == iota((BATCH, BATCH), 1)
    logits = jnp.where(everyone, -1e30, logits)
    lse_all = shift + jnp.log(jnp.sum(jnp.exp(logits - shift), axis=0, keepdims=True))
    at = pl.ds(pl.multiple_of(first, 8), 8)
    own = (gram_ref[0, at, :] + gram_ref[1, at, :]) * inv_tau
    own = jnp.where(lane == mine, -1e30, own)
    lse = shift + jnp.log(jnp.sum(jnp.exp(own - shift), axis=1, keepdims=True))
    hits = lane == own_partner
    loss = lse - jnp.sum(jnp.where(hits, own, 0.0), axis=1, keepdims=True)
    as_query = loss_scale * (jnp.exp(own - lse) - jnp.where(hits, 1.0, 0.0))
    as_key = loss_scale * (jnp.exp(own - lse_all) - jnp.where(partner == mine, 1.0, 0.0))
    weights = jnp.concatenate([as_query, as_key], axis=0).astype(BF16)
    grad = jnp.dot(weights, unit_ref[...], preferred_element_type=F32)
    grad = (grad[0:8] + grad[8:16]) * inv_tau
    weights = weights.astype(F32)
    length = length_ref[:, 0:1]
    along = (gram_ref[0, BATCH:] + gram_ref[1, BATCH:]) / length
    inner = inv_tau * jnp.sum((weights[0:8] + weights[8:16]) * along, axis=1, keepdims=True)
    grad = ((grad - embed_ref[...] / length * inner) / length).astype(BF16)
    for peer in range(N_DP):
        send_ref[peer] = grad
    place = (iota((8, 128), 1) + core * PAS) == iota((8, 128), 0)
    loss = jnp.sum(jnp.where(place, loss, 0.0), axis=0, keepdims=True)
    loss_ref[...] = loss[:, 0:PAS]


def rows_kernel(
    grad_ref, hidden_ref, segment_ref, assign_ref, gain_ref, upright_ref, out_hbm,
    scaled, coef, out, sems,
):
    core = lax.axis_index("core")
    row = iota((8, N_DP * 8), 0)
    lane = iota((8, N_DP * 8), 1)
    select = jnp.zeros((8, N_DP * 8), F32)
    for k in range(PAS):
        owner = assign_ref[0, k]
        at = lax.div(owner, PAS) * 8 + core * PAS + lax.rem(owner, PAS)
        select = jnp.where((row == k) & (lane == at), 1.0, select)
    select = select.astype(BF16)
    segment = jnp.broadcast_to(segment_ref[0], (8, ROWS))
    onehot = jnp.where(segment == iota((8, ROWS), 0), 1.0, 0.0)
    counts = jnp.maximum(jnp.sum(onehot, axis=1, keepdims=True), 1.0)
    for h in range(2):
        columns = pl.ds(h * HALF, HALF)
        part = jnp.dot(select, grad_ref[h], preferred_element_type=F32)
        scaled[:, columns] = split3(gain_ref[:, columns] * (part / counts))
    upright = upright_ref[...]
    spread = upright[:, 0:24]
    inverse = upright[:, 24:25]
    dots = lax.dot_general(
        hidden_ref[0], scaled[...], (((1,), (1,)), ((), ())), preferred_element_type=F32
    )
    dot = jnp.sum(dots * spread, axis=1, keepdims=True) * (1.0 / D)
    coef[:, 0:128] = jnp.broadcast_to(inverse, (ROWS, 128))
    coef[:, 128:256] = jnp.broadcast_to(inverse * inverse * inverse * dot, (ROWS, 128))
    spread = spread.astype(BF16)
    width = 512
    copies = []
    for at in range(0, D, width):
        columns = pl.ds(at, width)
        gained = jnp.dot(spread, scaled[:, columns], preferred_element_type=F32)
        values = hidden_ref[0, :, columns].astype(F32)
        out[:, columns] = (coef[:, 0:1] * gained - values * coef[:, 128:129]).astype(BF16)
        copy = pltpu.make_async_copy(
            out.at[:, columns], out_hbm.at[0, :, columns], sems.at[at // width]
        )
        copy.start()
        copies.append(copy)
    for copy in copies:
        copy.wait()


def local(hidden, segment_ids, assign, positive, gain):
    shape = jax.ShapeDtypeStruct
    gain = gain.reshape(1, D)
    with jax.named_scope("pool"):
        send, upright, partner = pl.pallas_call(
            pool_kernel,
            out_shape=(
                shape((N_DP, 8, HALF), BF16),
                shape((ROWS, 128), F32),
                shape((1, BATCH), jnp.int32),
            ),
            in_specs=[HBM] * 5,
            out_specs=(VMEM, VMEM, VMEM),
            scratch_shapes=[
                pltpu.VMEM((ROWS, D), BF16),
                pltpu.VMEM((1, 1, ROWS), jnp.int32),
                pltpu.VMEM((1, PAS), jnp.int32),
                pltpu.VMEM((1, D), F32),
                pltpu.VMEM((PAS, 64), jnp.int32),
                pltpu.VMEM((ROWS, 128), F32),
                pltpu.SemaphoreType.DMA((ROWS // CHUNK,)),
                pltpu.SemaphoreType.DMA((4,)),
            ],
            compiler_params=PARAMS,
        )(*[pltpu.with_memory_space_constraint(v, pltpu.HBM) for v in (hidden, segment_ids, assign, gain, positive.T)])
    with jax.named_scope("pooled_exchange"):
        pooled = lax.all_gather(lax.all_to_all(send, "dp", 0, 0), "core", axis=0)
    with jax.named_scope("unit"):
        send, embed, length = pl.pallas_call(
            unit_kernel,
            out_shape=(shape((N_XY, 8, HALF), BF16), shape((8, HALF), F32), shape((8, 128), F32)),
            in_specs=[VMEM],
            out_specs=(VMEM, VMEM, VMEM),
            compiler_params=PARAMS,
        )(pooled)
    with jax.named_scope("unit_exchange"):
        units = lax.all_to_all(send, ("x", "y"), 0, 0).reshape(BATCH, HALF)
    with jax.named_scope("gram"):
        gram = pl.pallas_call(
            gram_kernel,
            out_shape=shape((BATCH + 8, BATCH), F32),
            in_specs=[VMEM, VMEM],
            out_specs=VMEM,
            compiler_params=PARAMS,
        )(units, embed)
        gram = lax.all_gather(gram, "core", axis=0)
    with jax.named_scope("contrast"):
        loss, send = pl.pallas_call(
            contrast_kernel,
            out_shape=(shape((1, PAS), F32), shape((N_DP, 8, HALF), BF16)),
            in_specs=[VMEM] * 5,
            out_specs=(VMEM, VMEM),
            compiler_params=PARAMS,
        )(gram, units, embed, length, partner)
    with jax.named_scope("grad_exchange"):
        grads = lax.all_to_all(send, "dp", 0, 0)
        grads = lax.all_gather(grads.reshape(N_DP * 8, HALF), "core", axis=0)
    with jax.named_scope("rows"):
        grad_rows = pl.pallas_call(
            rows_kernel,
            out_shape=shape((1, ROWS, D), BF16),
            in_specs=[VMEM, VMEM, VMEM, SMEM, VMEM, VMEM],
            out_specs=HBM,
            scratch_shapes=[
                pltpu.VMEM((24, D), BF16),
                pltpu.VMEM((ROWS, 256), F32),
                pltpu.VMEM((ROWS, D), BF16),
                pltpu.SemaphoreType.DMA((8,)),
            ],
            compiler_params=PARAMS,
        )(grads, hidden, segment_ids, assign, gain, upright)
    return loss, grad_rows


def solution(mesh):
    fine = Mesh(mesh.devices.reshape(4, 8, 2, N_DP), ("x", "y", "core", "dp"))
    group = ("x", "y", "core")
    placed = (P(group, "dp", None), P(group, "dp", None), P(group, "dp"), P(None, "dp"), P())
    return jax.shard_map(
        local,
        mesh=fine,
        in_specs=placed,
        out_specs=(P(group, "dp"), P(group, "dp", None)),
        check_vma=False,
    )
```

```python
import functools

import jax
import jax.numpy as jnp
from jax import lax
from jax.experimental import pallas as pl
from jax.experimental.pallas import tpu as pltpu
from jax.sharding import Mesh
from jax.sharding import PartitionSpec as P

inv_tau = 20.0
loss_scale = 1024.0
norm_eps = 1e-06

F32 = jnp.float32
BF16 = jnp.bfloat16
ROWS = 256
D = 4096
HALF = D // 2
QUARTER = D // 4
PAS = 4
CHUNK = 64
N_DP = 12
N_X = 4
N_Y = 8
BATCH = 256

VMEM = pl.BlockSpec(memory_space=pltpu.VMEM)
SMEM = pl.BlockSpec(memory_space=pltpu.SMEM)
HBM = pl.BlockSpec(memory_space=pltpu.HBM)
PARAMS = pltpu.CompilerParams(vmem_limit_bytes=40 * 1024 * 1024)


def iota(shape, dim):
    return lax.broadcasted_iota(jnp.int32, shape, dim)


def split3(values):
    high = values.astype(BF16).astype(F32)
    rest = values - high
    middle = rest.astype(BF16).astype(F32)
    low = rest - middle
    return jnp.concatenate([high, middle, low], axis=0).astype(BF16)


def sum3(values):
    return values[0:8] + values[8:16] + values[16:24]


def pool_kernel(
    hidden_hbm, segment_hbm, assign_hbm, gain_hbm, positive_hbm,
    send_ref, upright_ref, partner_ref,
    hidden, segment_at, assign_at, gain, positive, sums, chunk_sem, small_sem,
):
    chunks = [pl.ds(at * CHUNK, CHUNK) for at in range(ROWS // CHUNK)]
    copies = [
        pltpu.make_async_copy(hidden_hbm.at[0, rows], hidden.at[rows], chunk_sem.at[at])
        for at, rows in enumerate(chunks)
    ]
    small = [
        pltpu.make_async_copy(source, target, small_sem.at[at])
        for at, (source, target) in enumerate(
            [(segment_hbm, segment_at), (assign_hbm, assign_at), (positive_hbm, positive), (gain_hbm, gain)]
        )
    ]
    copies[0].start()
    for copy in small:
        copy.start()
    for copy in copies[1:]:
        copy.start()

    for copy in small:
        copy.wait()
    segment = jnp.broadcast_to(segment_at[0], (8, ROWS))
    onehot = jnp.where(segment == iota((8, ROWS), 0), 1.0, 0.0)
    counts = jnp.maximum(jnp.sum(onehot, axis=1, keepdims=True), 1.0)
    row = iota((N_DP * 8, 8), 0)
    lane = iota((N_DP * 8, 8), 1)
    owner = jnp.zeros((N_DP * 8, 8), jnp.int32)
    for k in range(PAS):
        owner = jnp.where(lax.rem(lane, PAS) == k, assign_at[0:1, k : k + 1], owner)
    slot = lax.div(row, 8) * PAS + lax.rem(row, PAS)
    place = (owner == slot) & (lax.div(lax.rem(row, 8), PAS) == lax.div(lane, PAS))
    place = jnp.where(place, 1.0, 0.0).astype(BF16)
    lane = iota((64, BATCH), 1)
    spread = jnp.where(lax.div(lane, PAS) == iota((64, BATCH), 0), 1.0, 0.0).astype(BF16)
    partner = jnp.concatenate([positive[...].astype(F32), jnp.zeros((PAS, 64), F32)], axis=0)
    partner = jnp.dot(partner.astype(BF16), spread, preferred_element_type=F32)
    partner = jnp.where(lax.rem(iota((8, BATCH), 1), PAS) == iota((8, BATCH), 0), partner, 0.0)
    partner_ref[...] = jnp.sum(partner, axis=0, keepdims=True).astype(jnp.int32)

    for at in range(ROWS // CHUNK):
        copies[at].wait()

        def block(step, carry):
            rows = pl.ds(pl.multiple_of(at * CHUNK + step * 16, 16), 16)
            values = hidden[rows, :].astype(F32)
            total = jnp.sum(values * values, axis=1, keepdims=True)
            sums[rows, :] = jnp.broadcast_to(total, (16, 128))
            return carry

        lax.fori_loop(0, CHUNK // 16, block, 0)
    inverse = lax.rsqrt(sums[...].T[0:8] * (1.0 / D) + norm_eps)
    weights = split3(onehot * inverse)
    for h in range(2):
        columns = pl.ds(h * HALF, HALF)
        pooled = sum3(jnp.dot(weights, hidden[:, columns], preferred_element_type=F32))
        pooled = (pooled * gain[:, columns] / counts)[0:PAS]
        pooled = jnp.concatenate([pooled[:, 0:QUARTER], pooled[:, QUARTER:]], axis=0).astype(BF16)
        placed = jnp.dot(place, pooled, preferred_element_type=F32).astype(BF16)
        send_ref[h] = placed.reshape(N_DP, 8, QUARTER)
    upright_ref[...] = jnp.concatenate(
        [onehot, onehot, onehot, inverse, jnp.zeros((96, ROWS), F32)], axis=0
    ).T


def owned_kernel(pooled_ref, send_ref, embed_ref):
    embeds = []
    for c in range(2):
        embed = pooled_ref[c, 0].astype(F32)
        for peer in range(1, N_DP):
            embed = embed + pooled_ref[c, peer].astype(F32)
        embeds.append(jnp.concatenate([embed[0:PAS], embed[PAS:]], axis=1))
    own = jnp.concatenate(embeds, axis=0)
    embed_ref[...] = own
    own = own.astype(BF16)
    for peer in range(N_Y):
        send_ref[peer] = own


def gram_kernel(embed_ref, gram_ref):
    embeds = embed_ref[...]
    gram_ref[...] = lax.dot_general(
        embeds, embeds, (((1,), (1,)), ((), ())), preferred_element_type=F32
    )


def contrast_kernel(gram_ref, batch_ref, embed_ref, partner_ref, loss_ref, send_ref):
    core = lax.axis_index("core")
    first = (lax.axis_index("x") * 8 + lax.axis_index("y")) * 8
    shift = inv_tau
    row = iota((8, BATCH), 0)
    lane = iota((8, BATCH), 1)
    mine = first + row
    partner = partner_ref[...]
    own_partner = jnp.sum(jnp.where(lane == mine, partner, 0), axis=1, keepdims=True)

    gram = gram_ref[0] + gram_ref[1]
    everyone = iota((BATCH, BATCH), 0) == iota((BATCH, BATCH), 1)
    diagonal = jnp.where(everyone, gram, 0.0)
    across = lax.rsqrt(jnp.sum(diagonal, axis=0, keepdims=True) + norm_eps)
    down = lax.rsqrt(jnp.sum(diagonal, axis=1, keepdims=True) + norm_eps)
    logits = jnp.where(everyone, -1e30, gram * down * across * inv_tau)
    lse_all = shift + jnp.log(jnp.sum(jnp.exp(logits - shift), axis=0, keepdims=True))
    at = pl.ds(pl.multiple_of(first, 8), 8)
    own = gram_ref[0, at, :] + gram_ref[1, at, :]
    scale = lax.rsqrt(
        jnp.sum(jnp.where(lane == mine, own, 0.0), axis=1, keepdims=True) + norm_eps
    )
    cosine = own * scale * across
    own = jnp.where(lane == mine, -1e30, cosine * inv_tau)
    lse = shift + jnp.log(jnp.sum(jnp.exp(own - shift), axis=1, keepdims=True))
    hits = lane == own_partner
    loss = lse - jnp.sum(jnp.where(hits, own, 0.0), axis=1, keepdims=True)
    as_query = loss_scale * (jnp.exp(own - lse) - jnp.where(hits, 1.0, 0.0))
    as_key = loss_scale * (jnp.exp(own - lse_all) - jnp.where(partner == mine, 1.0, 0.0))
    weights = as_query.astype(BF16).astype(F32) + as_key.astype(BF16).astype(F32)
    inner = inv_tau * jnp.sum(weights * cosine, axis=1, keepdims=True)
    grad = jnp.dot(split3(weights * across), batch_ref[...], preferred_element_type=F32)
    grad = (sum3(grad) * inv_tau - embed_ref[...] * (scale * inner)) * scale
    for c in range(2):
        part = grad[c * PAS : (c + 1) * PAS]
        part = jnp.concatenate([part[:, 0:QUARTER], part[:, QUARTER:]], axis=0).astype(BF16)
        for peer in range(N_DP):
            send_ref[c, peer] = part
    place = (iota((8, 128), 1) + core * PAS) == iota((8, 128), 0)
    loss = jnp.sum(jnp.where(place, loss, 0.0), axis=0, keepdims=True)
    loss_ref[...] = loss[:, 0:PAS]


def rows_kernel(
    grad_ref, hidden_ref, segment_ref, assign_ref, gain_ref, upright_ref, out_hbm,
    scaled, coef, out, sems,
):
    row = iota((8, N_DP * 8), 0)
    lane = iota((8, N_DP * 8), 1)
    select = jnp.zeros((8, N_DP * 8), F32)
    for k in range(PAS):
        owner = assign_ref[0, k]
        at = lax.div(owner, PAS) * 8 + lax.rem(owner, PAS) + lax.div(row, PAS) * PAS
        select = jnp.where((lax.rem(row, PAS) == k) & (lane == at), 1.0, select)
    select = select.astype(BF16)
    segment = jnp.broadcast_to(segment_ref[0], (8, ROWS))
    onehot = jnp.where(segment == iota((8, ROWS), 0), 1.0, 0.0)
    counts = jnp.maximum(jnp.sum(onehot, axis=1, keepdims=True), 1.0)
    for h in range(2):
        part = jnp.dot(select, grad_ref[h], preferred_element_type=F32)
        for q in range(2):
            columns = pl.ds((h * 2 + q) * QUARTER, QUARTER)
            scaled[:, columns] = split3(gain_ref[:, columns] * (part / counts))
            part = jnp.concatenate([part[PAS:], part[0:PAS]], axis=0)
    upright = upright_ref[...]
    spread = upright[:, 0:24]
    inverse = upright[:, 24:25]
    dots = lax.dot_general(
        hidden_ref[0], scaled[...], (((1,), (1,)), ((), ())), preferred_element_type=F32
    )
    dot = jnp.sum(dots * spread, axis=1, keepdims=True) * (1.0 / D)
    coef[:, 0:128] = jnp.broadcast_to(inverse, (ROWS, 128))
    coef[:, 128:256] = jnp.broadcast_to(inverse * inverse * inverse * dot, (ROWS, 128))
    spread = spread.astype(BF16)
    width = 512
    copies = []
    for at in range(0, D, width):
        columns = pl.ds(at, width)
        gained = jnp.dot(spread, scaled[:, columns], preferred_element_type=F32)
        values = hidden_ref[0, :, columns].astype(F32)
        out[:, columns] = (coef[:, 0:1] * gained - values * coef[:, 128:129]).astype(BF16)
        copy = pltpu.make_async_copy(
            out.at[:, columns], out_hbm.at[0, :, columns], sems.at[at // width]
        )
        copy.start()
        copies.append(copy)
    for copy in copies:
        copy.wait()


def local(hidden, segment_ids, assign, positive, gain):
    shape = jax.ShapeDtypeStruct
    gain = gain.reshape(1, D)
    with jax.named_scope("pool"):
        send, upright, partner = pl.pallas_call(
            pool_kernel,
            out_shape=(
                shape((2, N_DP, 8, QUARTER), BF16),
                shape((ROWS, 128), F32),
                shape((1, BATCH), jnp.int32),
            ),
            in_specs=[HBM] * 5,
            out_specs=(VMEM, VMEM, VMEM),
            scratch_shapes=[
                pltpu.VMEM((ROWS, D), BF16),
                pltpu.VMEM((1, 1, ROWS), jnp.int32),
                pltpu.VMEM((1, PAS), jnp.int32),
                pltpu.VMEM((1, D), F32),
                pltpu.VMEM((PAS, 64), jnp.int32),
                pltpu.VMEM((ROWS, 128), F32),
                pltpu.SemaphoreType.DMA((ROWS // CHUNK,)),
                pltpu.SemaphoreType.DMA((4,)),
            ],
            compiler_params=PARAMS,
        )(*[pltpu.with_memory_space_constraint(v, pltpu.HBM) for v in (hidden, segment_ids, assign, gain, positive.T)])
    with jax.named_scope("pooled_exchange"):
        pooled = lax.all_to_all(send.reshape(2 * N_DP, 8, -1), ("core", "dp"), 0, 0)
        pooled = pooled.reshape(2, N_DP, 8, -1)
    with jax.named_scope("owned"):
        send, embed = pl.pallas_call(
            owned_kernel,
            out_shape=(shape((N_Y, 8, HALF), BF16), shape((8, HALF), F32)),
            in_specs=[VMEM],
            out_specs=(VMEM, VMEM),
            compiler_params=PARAMS,
        )(pooled)
    with jax.named_scope("embed_exchange"):
        batch = lax.all_to_all(send, "y", 0, 0).reshape(N_Y * 8, HALF)
        batch = jnp.broadcast_to(batch, (N_X, N_Y * 8, HALF))
        batch = lax.all_to_all(batch, "x", 0, 0).reshape(BATCH, HALF)
    with jax.named_scope("gram"):
        gram = pl.pallas_call(
            gram_kernel,
            out_shape=shape((BATCH, BATCH), F32),
            in_specs=[VMEM],
            out_specs=VMEM,
            compiler_params=PARAMS,
        )(batch)
        gram = lax.all_gather(gram, "core", axis=0)
    with jax.named_scope("contrast"):
        loss, send = pl.pallas_call(
            contrast_kernel,
            out_shape=(shape((1, PAS), F32), shape((2, N_DP, 8, QUARTER), BF16)),
            in_specs=[VMEM] * 4,
            out_specs=(VMEM, VMEM),
            compiler_params=PARAMS,
        )(gram, batch, embed, partner)
    with jax.named_scope("grad_exchange"):
        grads = lax.all_to_all(send.reshape(2 * N_DP, 8, QUARTER), ("core", "dp"), 0, 0)
        grads = grads.reshape(2, N_DP * 8, QUARTER)
    with jax.named_scope("rows"):
        grad_rows = pl.pallas_call(
            rows_kernel,
            out_shape=shape((1, ROWS, D), BF16),
            in_specs=[VMEM, VMEM, VMEM, SMEM, VMEM, VMEM],
            out_specs=HBM,
            scratch_shapes=[
                pltpu.VMEM((24, D), BF16),
                pltpu.VMEM((ROWS, 256), F32),
                pltpu.VMEM((ROWS, D), BF16),
                pltpu.SemaphoreType.DMA((8,)),
            ],
            compiler_params=PARAMS,
        )(grads, hidden, segment_ids, assign, gain, upright)
    return loss, grad_rows


def solution(mesh):
    fine = Mesh(mesh.devices.reshape(4, 8, 2, N_DP), ("x", "y", "core", "dp"))
    group = ("x", "y", "core")
    placed = (P(group, "dp", None), P(group, "dp", None), P(group, "dp"), P(None, "dp"), P())
    return jax.shard_map(
        local,
        mesh=fine,
        in_specs=placed,
        out_specs=(P(group, "dp"), P(group, "dp", None)),
        check_vma=False,
    )
```

```python
import functools

import jax
import jax.numpy as jnp
from jax import lax
from jax.experimental import pallas as pl
from jax.experimental.pallas import tpu as pltpu
from jax.sharding import Mesh
from jax.sharding import PartitionSpec as P

inv_tau = 20.0
loss_scale = 1024.0
norm_eps = 1e-06

F32 = jnp.float32
BF16 = jnp.bfloat16
ROWS = 256
D = 4096
HALF = D // 2
QUARTER = D // 4
PAS = 4
CHUNK = 1024
META = 128
N_ZH = 3
N_ZL = 4
N_X = 4
N_Y = 8
BATCH = 256

VMEM = pl.BlockSpec(memory_space=pltpu.VMEM)
HBM = pl.BlockSpec(memory_space=pltpu.HBM)
PARAMS = pltpu.CompilerParams(vmem_limit_bytes=40 * 1024 * 1024)


def iota(shape, dim):
    return lax.broadcasted_iota(jnp.int32, shape, dim)


def split3(values):
    high = values.astype(BF16).astype(F32)
    rest = values - high
    middle = rest.astype(BF16).astype(F32)
    low = rest - middle
    return jnp.concatenate([high, middle, low], axis=0).astype(BF16)


def sum3(values):
    return values[0:8] + values[8:16] + values[16:24]


def pool_kernel(
    hidden_hbm, segment_hbm, assign_hbm, gain_hbm, positive_hbm,
    send_ref, upright_ref, partner_ref,
    hidden, segment_at, assign_at, gain, positive, chunk_sem, small_sem,
):
    chunks = [pl.ds(at * CHUNK, CHUNK) for at in range(D // CHUNK)]
    copies = [
        pltpu.make_async_copy(hidden_hbm.at[0, :, part], hidden.at[:, part], chunk_sem.at[at])
        for at, part in enumerate(chunks)
    ]
    small = [
        pltpu.make_async_copy(source, target, small_sem.at[at])
        for at, (source, target) in enumerate(
            [(segment_hbm, segment_at), (assign_hbm, assign_at), (positive_hbm, positive), (gain_hbm, gain)]
        )
    ]
    copies[0].start()
    for copy in small:
        copy.start()
    for copy in copies[1:]:
        copy.start()

    for copy in small:
        copy.wait()
    segment = jnp.broadcast_to(segment_at[0], (8, ROWS))
    onehot = jnp.where(segment == iota((8, ROWS), 0), 1.0, 0.0)
    counts = jnp.maximum(jnp.sum(onehot, axis=1, keepdims=True), 1.0)
    row = iota((8, META), 0)
    owner = jnp.zeros((8, META), jnp.int32)
    for k in range(PAS):
        owner = jnp.where(lax.rem(row, PAS) == k, assign_at[0:1, k : k + 1], owner)
    place = lax.axis_index("core") * 32 + lax.axis_index("zl") * 8 + row
    meta = jnp.where(iota((8, META), 1) == place, owner, 0).astype(F32).astype(BF16)
    for h in range(2):
        for peer in range(N_ZL):
            send_ref[h, peer, :, QUARTER:] = meta
    lane = iota((64, BATCH), 1)
    spread = jnp.where(lax.div(lane, PAS) == iota((64, BATCH), 0), 1.0, 0.0).astype(BF16)
    partner = jnp.concatenate([positive[...].astype(F32), jnp.zeros((PAS, 64), F32)], axis=0)
    partner = jnp.dot(partner.astype(BF16), spread, preferred_element_type=F32)
    partner = jnp.where(lax.rem(iota((8, BATCH), 1), PAS) == iota((8, BATCH), 0), partner, 0.0)
    partner_ref[...] = jnp.sum(partner, axis=0, keepdims=True).astype(jnp.int32)

    products = jnp.zeros((ROWS, ROWS), F32)
    for at, part in enumerate(chunks):
        copies[at].wait()
        values = hidden[:, part]
        products = products + lax.dot_general(
            values, values, (((1,), (1,)), ((), ())), preferred_element_type=F32
        )
    products = jnp.where(iota((ROWS, ROWS), 0) == iota((ROWS, ROWS), 1), products, 0.0)
    squares = jnp.sum(products, axis=0, keepdims=True)
    inverse = jnp.broadcast_to(lax.rsqrt(squares * (1.0 / D) + norm_eps), (8, ROWS))
    weights = split3(onehot * inverse)
    for h in range(2):
        columns = pl.ds(h * HALF, HALF)
        pooled = sum3(jnp.dot(weights, hidden[:, columns], preferred_element_type=F32))
        pooled = (pooled * gain[:, columns] / counts)[0:PAS]
        pooled = jnp.concatenate([pooled[:, 0:QUARTER], pooled[:, QUARTER:]], axis=0).astype(BF16)
        for peer in range(N_ZL):
            send_ref[h, peer, :, 0:QUARTER] = pooled
    upright_ref[...] = jnp.concatenate(
        [onehot, onehot, onehot, inverse, jnp.zeros((96, ROWS), F32)], axis=0
    ).T


def relay_kernel(pooled_ref, send_ref, back_ref):
    relay = lax.axis_index("zl")
    owners = jnp.sum(pooled_ref[:, QUARTER:].astype(F32), axis=0, keepdims=True)
    row = iota((128, META), 0)
    lane = iota((128, META), 1)
    slot = (lax.div(row, 8) * N_ZL + relay) * PAS + lax.rem(row, PAS)
    hit = (owners == slot.astype(F32)) & (lax.div(lane, 32) == lax.div(lax.rem(row, 8), PAS))
    hit = hit & (row < N_ZH * 8) & (lane < 64)
    select = jnp.where(hit, 1.0, 0.0)
    back_ref[...] = select.T
    pooled = pooled_ref[:, 0:QUARTER]
    for q in range(2):
        part = jnp.where(lax.rem(lax.div(lane, PAS), 2) == q, select, 0.0)[0 : N_ZH * 8, 0:64]
        kept = jnp.dot(part.astype(BF16), pooled, preferred_element_type=F32)
        for peer in range(N_ZH):
            send_ref[peer, :, q * QUARTER : (q + 1) * QUARTER] = kept[
                peer * 8 : (peer + 1) * 8
            ].astype(BF16)


def owned_kernel(pooled_ref, send_ref, embed_ref):
    own = pooled_ref[0].astype(F32)
    for peer in range(1, N_ZH):
        own = own + pooled_ref[peer].astype(F32)
    embed_ref[...] = own
    own = own.astype(BF16)
    for peer in range(N_Y):
        send_ref[peer] = own


def gram_kernel(embed_ref, gram_ref):
    embeds = embed_ref[...]
    gram_ref[...] = lax.dot_general(
        embeds, embeds, (((1,), (1,)), ((), ())), preferred_element_type=F32
    )


def contrast_kernel(gram_ref, batch_ref, embed_ref, partner_ref, loss_ref, send_ref):
    core = lax.axis_index("core")
    first = (lax.axis_index("x") * 8 + lax.axis_index("y")) * 8
    shift = inv_tau
    row = iota((8, BATCH), 0)
    lane = iota((8, BATCH), 1)
    mine = first + row
    partner = partner_ref[...]
    own_partner = jnp.sum(jnp.where(lane == mine, partner, 0), axis=1, keepdims=True)

    gram = gram_ref[0] + gram_ref[1]
    everyone = iota((BATCH, BATCH), 0) == iota((BATCH, BATCH), 1)
    diagonal = jnp.where(everyone, gram, 0.0)
    across = lax.rsqrt(jnp.sum(diagonal, axis=0, keepdims=True) + norm_eps)
    down = lax.rsqrt(jnp.sum(diagonal, axis=1, keepdims=True) + norm_eps)
    logits = jnp.where(everyone, -1e30, gram * down * across * inv_tau)
    lse_all = shift + jnp.log(jnp.sum(jnp.exp(logits - shift), axis=0, keepdims=True))
    at = pl.ds(pl.multiple_of(first, 8), 8)
    own = gram_ref[0, at, :] + gram_ref[1, at, :]
    scale = lax.rsqrt(
        jnp.sum(jnp.where(lane == mine, own, 0.0), axis=1, keepdims=True) + norm_eps
    )
    cosine = own * scale * across
    own = jnp.where(lane == mine, -1e30, cosine * inv_tau)
    lse = shift + jnp.log(jnp.sum(jnp.exp(own - shift), axis=1, keepdims=True))
    hits = lane == own_partner
    loss = lse - jnp.sum(jnp.where(hits, own, 0.0), axis=1, keepdims=True)
    as_query = loss_scale * (jnp.exp(own - lse) - jnp.where(hits, 1.0, 0.0))
    as_key = loss_scale * (jnp.exp(own - lse_all) - jnp.where(partner == mine, 1.0, 0.0))
    weights = as_query.astype(BF16).astype(F32) + as_key.astype(BF16).astype(F32)
    inner = inv_tau * jnp.sum(weights * cosine, axis=1, keepdims=True)
    pair = jnp.concatenate([as_query, as_key], axis=0).astype(BF16)
    width = 512
    for start in range(0, HALF, width):
        columns = pl.ds(start, width)
        units = (batch_ref[:, columns].astype(F32) * down).astype(BF16)
        grad = jnp.dot(pair, units, preferred_element_type=F32)
        grad = (grad[0:8] + grad[8:16]) * inv_tau - embed_ref[:, columns] * (scale * inner)
        grad = (grad * scale).astype(BF16)
        for peer in range(N_ZH):
            send_ref[peer, :, columns] = grad
    place = (iota((8, 128), 1) + core * PAS) == iota((8, 128), 0)
    loss = jnp.sum(jnp.where(place, loss, 0.0), axis=0, keepdims=True)
    loss_ref[...] = loss[:, 0:PAS]


def back_kernel(grad_ref, back_ref, send_ref):
    back = back_ref[...]
    row = iota((128, META), 0)
    total = jnp.zeros((64, QUARTER), F32)
    for q in range(2):
        part = jnp.where(lax.rem(lax.div(row, PAS), 2) == q, back, 0.0)[0:64, 0 : N_ZH * 8]
        total = total + jnp.dot(
            part.astype(BF16),
            grad_ref[:, q * QUARTER : (q + 1) * QUARTER],
            preferred_element_type=F32,
        )
    total = total.astype(BF16)
    for c in range(2):
        for peer in range(N_ZL):
            at = (c * N_ZL + peer) * 8
            send_ref[c, peer] = total[at : at + 8]


def rows_kernel(
    grad_ref, hidden_ref, segment_ref, gain_ref, upright_ref, out_hbm,
    scaled, coef, out, sems, gained_ref,
):
    segment = jnp.broadcast_to(segment_ref[0], (8, ROWS))
    onehot = jnp.where(segment == iota((8, ROWS), 0), 1.0, 0.0)
    counts = jnp.maximum(jnp.sum(onehot, axis=1, keepdims=True), 1.0)
    for h in range(2):
        part = grad_ref[h, 0].astype(F32)
        for peer in range(1, N_ZL):
            part = part + grad_ref[h, peer].astype(F32)
        for q in range(2):
            columns = pl.ds((h * 2 + q) * QUARTER, QUARTER)
            scaled[:, columns] = split3(gain_ref[:, columns] * (part / counts))
            part = jnp.concatenate([part[PAS:], part[0:PAS]], axis=0)
    upright = upright_ref[...]
    spread = upright[:, 0:24]
    inverse = upright[:, 24:25]
    low = spread.astype(BF16)
    width = 512
    total = jnp.zeros((ROWS, 128), F32)
    for at in range(0, D, width):
        columns = pl.ds(at, width)
        part = jnp.dot(low, scaled[:, columns], preferred_element_type=F32)
        gained_ref[:, columns] = part
        part = part * hidden_ref[0, :, columns].astype(F32)
        for piece in range(0, width, 128):
            total = total + part[:, piece : piece + 128]
    dot = jnp.sum(total, axis=1, keepdims=True) * (1.0 / D)
    coef[:, 0:128] = jnp.broadcast_to(inverse, (ROWS, 128))
    coef[:, 128:256] = jnp.broadcast_to(inverse * inverse * inverse * dot, (ROWS, 128))
    copies = []
    for at in range(0, D, width):
        columns = pl.ds(at, width)
        gained = gained_ref[:, columns]
        values = hidden_ref[0, :, columns].astype(F32)
        out[:, columns] = (coef[:, 0:1] * gained - values * coef[:, 128:129]).astype(BF16)
        copy = pltpu.make_async_copy(
            out.at[:, columns], out_hbm.at[0, :, columns], sems.at[at // width]
        )
        copy.start()
        copies.append(copy)
    for copy in copies:
        copy.wait()


def local(hidden, segment_ids, assign, positive, gain):
    shape = jax.ShapeDtypeStruct
    gain = gain.reshape(1, D)
    with jax.named_scope("pool"):
        send, upright, partner = pl.pallas_call(
            pool_kernel,
            out_shape=(
                shape((2, N_ZL, 8, QUARTER + META), BF16),
                shape((ROWS, 128), F32),
                shape((1, BATCH), jnp.int32),
            ),
            in_specs=[HBM] * 5,
            out_specs=(VMEM, VMEM, VMEM),
            scratch_shapes=[
                pltpu.VMEM((ROWS, D), BF16),
                pltpu.VMEM((1, 1, ROWS), jnp.int32),
                pltpu.VMEM((1, PAS), jnp.int32),
                pltpu.VMEM((1, D), F32),
                pltpu.VMEM((PAS, 64), jnp.int32),
                pltpu.SemaphoreType.DMA((D // CHUNK,)),
                pltpu.SemaphoreType.DMA((4,)),
            ],
            compiler_params=PARAMS,
        )(*[pltpu.with_memory_space_constraint(v, pltpu.HBM) for v in (hidden, segment_ids, assign, gain, positive.T)])
    with jax.named_scope("pooled_to_relay"):
        pooled = lax.all_to_all(send.reshape(2 * N_ZL, 8, -1), ("core", "zl"), 0, 0)
        pooled = pooled.reshape(2 * N_ZL * 8, -1)
    with jax.named_scope("relay"):
        send, back = pl.pallas_call(
            relay_kernel,
            out_shape=(shape((N_ZH, 8, HALF), BF16), shape((128, META), F32)),
            in_specs=[VMEM],
            out_specs=(VMEM, VMEM),
            compiler_params=PARAMS,
        )(pooled)
    with jax.named_scope("pooled_to_owner"):
        pooled = lax.all_to_all(send, "zh", 0, 0)
    with jax.named_scope("owned"):
        send, embed = pl.pallas_call(
            owned_kernel,
            out_shape=(shape((N_Y, 8, HALF), BF16), shape((8, HALF), F32)),
            in_specs=[VMEM],
            out_specs=(VMEM, VMEM),
            compiler_params=PARAMS,
        )(pooled)
    with jax.named_scope("embed_exchange"):
        batch = lax.all_to_all(send, "y", 0, 0).reshape(N_Y * 8, HALF)
        batch = jnp.broadcast_to(batch, (N_X, N_Y * 8, HALF))
        batch = lax.all_to_all(batch, "x", 0, 0).reshape(BATCH, HALF)
    with jax.named_scope("gram"):
        gram = pl.pallas_call(
            gram_kernel,
            out_shape=shape((BATCH, BATCH), F32),
            in_specs=[VMEM],
            out_specs=VMEM,
            compiler_params=PARAMS,
        )(batch)
        gram = lax.all_gather(gram, "core", axis=0)
    with jax.named_scope("contrast"):
        loss, send = pl.pallas_call(
            contrast_kernel,
            out_shape=(shape((1, PAS), F32), shape((N_ZH, 8, HALF), BF16)),
            in_specs=[VMEM] * 4,
            out_specs=(VMEM, VMEM),
            compiler_params=PARAMS,
        )(gram, batch, embed, partner)
    with jax.named_scope("grad_to_relay"):
        grads = lax.all_to_all(send, "zh", 0, 0).reshape(N_ZH * 8, HALF)
    with jax.named_scope("back"):
        send = pl.pallas_call(
            back_kernel,
            out_shape=shape((2, N_ZL, 8, QUARTER), BF16),
            in_specs=[VMEM, VMEM],
            out_specs=VMEM,
            compiler_params=PARAMS,
        )(grads, back)
    with jax.named_scope("grad_to_rows"):
        grads = lax.all_to_all(send.reshape(2 * N_ZL, 8, QUARTER), ("core", "zl"), 0, 0)
        grads = grads.reshape(2, N_ZL, 8, QUARTER)
    with jax.named_scope("rows"):
        grad_rows = pl.pallas_call(
            rows_kernel,
            out_shape=shape((1, ROWS, D), BF16),
            in_specs=[VMEM] * 5,
            out_specs=HBM,
            scratch_shapes=[
                pltpu.VMEM((24, D), BF16),
                pltpu.VMEM((ROWS, 256), F32),
                pltpu.VMEM((ROWS, D), BF16),
                pltpu.SemaphoreType.DMA((8,)),
                pltpu.VMEM((ROWS, D), F32),
            ],
            compiler_params=PARAMS,
        )(grads, hidden, segment_ids, gain, upright)
    return loss, grad_rows


def solution(mesh):
    fine = Mesh(
        mesh.devices.reshape(N_X, N_Y, 2, N_ZH, N_ZL), ("x", "y", "core", "zh", "zl")
    )
    group, dp = ("x", "y", "core"), ("zh", "zl")
    placed = (P(group, dp, None), P(group, dp, None), P(group, dp), P(None, dp), P())
    return jax.shard_map(
        local,
        mesh=fine,
        in_specs=placed,
        out_specs=(P(group, dp), P(group, dp, None)),
        check_vma=False,
    )
```

```python
import functools

import jax
import jax.numpy as jnp
from jax import lax
from jax.experimental import pallas as pl
from jax.experimental.pallas import tpu as pltpu
from jax.sharding import Mesh
from jax.sharding import PartitionSpec as P

inv_tau = 20.0
loss_scale = 1024.0
norm_eps = 1e-06

F32 = jnp.float32
BF16 = jnp.bfloat16
ROWS = 256
D = 4096
HALF = D // 2
QUARTER = D // 4
PAS = 4
CHUNK = 1024
BLOCK = 64
META = 128
N_ZH = 3
N_ZL = 4
N_X = 4
N_Y = 8
BATCH = 256

VMEM = pl.BlockSpec(memory_space=pltpu.VMEM)
HBM = pl.BlockSpec(memory_space=pltpu.HBM)
PARAMS = pltpu.CompilerParams(vmem_limit_bytes=40 * 1024 * 1024)


def iota(shape, dim):
    return lax.broadcasted_iota(jnp.int32, shape, dim)


def split3(values):
    high = values.astype(BF16).astype(F32)
    rest = values - high
    middle = rest.astype(BF16).astype(F32)
    low = rest - middle
    return jnp.concatenate([high, middle, low], axis=0).astype(BF16)


def sum3(values):
    return values[0:8] + values[8:16] + values[16:24]


def pool_kernel(
    hidden_hbm, segment_hbm, assign_hbm, gain_hbm, positive_hbm,
    send_ref, upright_ref, partner_ref,
    hidden, segment_at, assign_at, gain, positive, chunk_sem, small_sem,
):
    chunks = [pl.ds(at * CHUNK, CHUNK) for at in range(D // CHUNK)]
    copies = [
        pltpu.make_async_copy(hidden_hbm.at[0, :, part], hidden.at[:, part], chunk_sem.at[at])
        for at, part in enumerate(chunks)
    ]
    small = [
        pltpu.make_async_copy(source, target, small_sem.at[at])
        for at, (source, target) in enumerate(
            [(segment_hbm, segment_at), (assign_hbm, assign_at), (positive_hbm, positive), (gain_hbm, gain)]
        )
    ]
    copies[0].start()
    for copy in small:
        copy.start()
    for copy in copies[1:]:
        copy.start()

    for copy in small:
        copy.wait()
    segment = jnp.broadcast_to(segment_at[0], (8, ROWS))
    onehot = jnp.where(segment == iota((8, ROWS), 0), 1.0, 0.0)
    counts = jnp.maximum(jnp.sum(onehot, axis=1, keepdims=True), 1.0)
    row = iota((8, META), 0)
    owner = jnp.zeros((8, META), jnp.int32)
    for k in range(PAS):
        owner = jnp.where(lax.rem(row, PAS) == k, assign_at[0:1, k : k + 1], owner)
    place = lax.axis_index("core") * 32 + lax.axis_index("zl") * 8 + row
    meta = jnp.where(iota((8, META), 1) == place, owner, 0).astype(F32).astype(BF16)
    for h in range(2):
        for peer in range(N_ZL):
            send_ref[h, peer, :, QUARTER:] = meta
    lane = iota((64, BATCH), 1)
    spread = jnp.where(lax.div(lane, PAS) == iota((64, BATCH), 0), 1.0, 0.0).astype(BF16)
    partner = jnp.concatenate([positive[...].astype(F32), jnp.zeros((PAS, 64), F32)], axis=0)
    partner = jnp.dot(partner.astype(BF16), spread, preferred_element_type=F32)
    partner = jnp.where(lax.rem(iota((8, BATCH), 1), PAS) == iota((8, BATCH), 0), partner, 0.0)
    partner_ref[...] = jnp.sum(partner, axis=0, keepdims=True).astype(jnp.int32)

    total = jnp.zeros((ROWS, 128), F32)
    for at, part in enumerate(chunks):
        copies[at].wait()
        for piece in range(0, CHUNK, 128):
            values = hidden[:, at * CHUNK + piece : at * CHUNK + piece + 128].astype(F32)
            total = total + values * values
    squares = jnp.sum(total.T, axis=0, keepdims=True)
    inverse = jnp.broadcast_to(lax.rsqrt(squares * (1.0 / D) + norm_eps), (8, ROWS))
    weights = split3(onehot * inverse)
    for h in range(2):
        columns = pl.ds(h * HALF, HALF)
        pooled = sum3(jnp.dot(weights, hidden[:, columns], preferred_element_type=F32))
        pooled = (pooled * gain[:, columns] / counts)[0:PAS]
        pooled = jnp.concatenate([pooled[:, 0:QUARTER], pooled[:, QUARTER:]], axis=0).astype(BF16)
        for peer in range(N_ZL):
            send_ref[h, peer, :, 0:QUARTER] = pooled
    upright_ref[...] = jnp.concatenate(
        [onehot, onehot, onehot, inverse, jnp.zeros((96, ROWS), F32)], axis=0
    ).T


def relay_kernel(pooled_ref, send_ref, back_ref):
    relay = lax.axis_index("zl")
    owners = jnp.sum(pooled_ref[:, QUARTER:].astype(F32), axis=0, keepdims=True)
    row = iota((128, META), 0)
    lane = iota((128, META), 1)
    slot = (lax.div(row, 8) * N_ZL + relay) * PAS + lax.rem(row, PAS)
    hit = (owners == slot.astype(F32)) & (lax.div(lane, 32) == lax.div(lax.rem(row, 8), PAS))
    hit = hit & (row < N_ZH * 8) & (lane < 64)
    select = jnp.where(hit, 1.0, 0.0)
    back_ref[...] = select.T
    pooled = pooled_ref[:, 0:QUARTER]
    for q in range(2):
        part = jnp.where(lax.rem(lax.div(lane, PAS), 2) == q, select, 0.0)[0 : N_ZH * 8, 0:64]
        kept = jnp.dot(part.astype(BF16), pooled, preferred_element_type=F32)
        for peer in range(N_ZH):
            send_ref[peer, :, q * QUARTER : (q + 1) * QUARTER] = kept[
                peer * 8 : (peer + 1) * 8
            ].astype(BF16)


def owned_kernel(pooled_ref, send_ref, embed_ref):
    own = pooled_ref[0].astype(F32)
    for peer in range(1, N_ZH):
        own = own + pooled_ref[peer].astype(F32)
    embed_ref[...] = own
    own = own.astype(BF16)
    for peer in range(N_Y):
        send_ref[peer] = own


def gram_kernel(embed_ref, gram_ref):
    embeds = embed_ref[...]
    gram_ref[...] = lax.dot_general(
        embeds, embeds, (((1,), (1,)), ((), ())), preferred_element_type=F32
    )


def contrast_kernel(gram_ref, batch_ref, embed_ref, partner_ref, loss_ref, send_ref):
    core = lax.axis_index("core")
    first = (lax.axis_index("x") * 8 + lax.axis_index("y")) * 8
    shift = inv_tau
    row = iota((8, BATCH), 0)
    lane = iota((8, BATCH), 1)
    mine = first + row
    partner = partner_ref[...]
    own_partner = jnp.sum(jnp.where(lane == mine, partner, 0), axis=1, keepdims=True)

    gram = gram_ref[0] + gram_ref[1]
    everyone = iota((BATCH, BATCH), 0) == iota((BATCH, BATCH), 1)
    diagonal = jnp.where(everyone, gram, 0.0)
    across = lax.rsqrt(jnp.sum(diagonal, axis=0, keepdims=True) + norm_eps)
    down = lax.rsqrt(jnp.sum(diagonal, axis=1, keepdims=True) + norm_eps)
    logits = jnp.where(everyone, -1e30, gram * down * across * inv_tau)
    lse_all = shift + jnp.log(jnp.sum(jnp.exp(logits - shift), axis=0, keepdims=True))
    at = pl.ds(pl.multiple_of(first, 8), 8)
    own = gram_ref[0, at, :] + gram_ref[1, at, :]
    scale = lax.rsqrt(
        jnp.sum(jnp.where(lane == mine, own, 0.0), axis=1, keepdims=True) + norm_eps
    )
    cosine = own * scale * across
    own = jnp.where(lane == mine, -1e30, cosine * inv_tau)
    lse = shift + jnp.log(jnp.sum(jnp.exp(own - shift), axis=1, keepdims=True))
    hits = lane == own_partner
    loss = lse - jnp.sum(jnp.where(hits, own, 0.0), axis=1, keepdims=True)
    as_query = loss_scale * (jnp.exp(own - lse) - jnp.where(hits, 1.0, 0.0))
    as_key = loss_scale * (jnp.exp(own - lse_all) - jnp.where(partner == mine, 1.0, 0.0))
    weights = as_query.astype(BF16).astype(F32) + as_key.astype(BF16).astype(F32)
    inner = inv_tau * jnp.sum(weights * cosine, axis=1, keepdims=True)
    pair = jnp.concatenate([as_query, as_key], axis=0).astype(BF16)
    width = 512
    for start in range(0, HALF, width):
        columns = pl.ds(start, width)
        units = (batch_ref[:, columns].astype(F32) * down).astype(BF16)
        grad = jnp.dot(pair, units, preferred_element_type=F32)
        grad = (grad[0:8] + grad[8:16]) * inv_tau - embed_ref[:, columns] * (scale * inner)
        grad = (grad * scale).astype(BF16)
        for peer in range(N_ZH):
            send_ref[peer, :, columns] = grad
    place = (iota((8, 128), 1) + core * PAS) == iota((8, 128), 0)
    loss = jnp.sum(jnp.where(place, loss, 0.0), axis=0, keepdims=True)
    loss_ref[...] = loss[:, 0:PAS]


def back_kernel(grad_ref, back_ref, send_ref):
    back = back_ref[...]
    row = iota((128, META), 0)
    total = jnp.zeros((64, QUARTER), F32)
    for q in range(2):
        part = jnp.where(lax.rem(lax.div(row, PAS), 2) == q, back, 0.0)[0:64, 0 : N_ZH * 8]
        total = total + jnp.dot(
            part.astype(BF16),
            grad_ref[:, q * QUARTER : (q + 1) * QUARTER],
            preferred_element_type=F32,
        )
    total = total.astype(BF16)
    for c in range(2):
        for peer in range(N_ZL):
            at = (c * N_ZL + peer) * 8
            send_ref[c, peer] = total[at : at + 8]


def rows_kernel(
    grad_ref, hidden_ref, segment_ref, gain_ref, upright_ref, out_hbm,
    scaled, gained, out, sems,
):
    segment = jnp.broadcast_to(segment_ref[0], (8, ROWS))
    onehot = jnp.where(segment == iota((8, ROWS), 0), 1.0, 0.0)
    counts = jnp.maximum(jnp.sum(onehot, axis=1, keepdims=True), 1.0)
    for h in range(2):
        part = grad_ref[h, 0].astype(F32)
        for peer in range(1, N_ZL):
            part = part + grad_ref[h, peer].astype(F32)
        for q in range(2):
            columns = pl.ds((h * 2 + q) * QUARTER, QUARTER)
            scaled[:, columns] = split3(gain_ref[:, columns] * (part / counts))
            part = jnp.concatenate([part[PAS:], part[0:PAS]], axis=0)
    width = 1024
    copies = []
    for start in range(0, ROWS, BLOCK):
        rows = pl.ds(start, BLOCK)
        spread = upright_ref[rows, 0:24].astype(BF16)
        inverse = upright_ref[rows, 24:25]
        total = jnp.zeros((BLOCK, 128), F32)
        for at in range(0, D, width):
            columns = pl.ds(at, width)
            part = jnp.dot(spread, scaled[:, columns], preferred_element_type=F32)
            gained[:, columns] = part
            part = part * hidden_ref[0, rows, columns].astype(F32)
            for piece in range(0, width, 128):
                total = total + part[:, piece : piece + 128]
        dot = jnp.sum(total, axis=1, keepdims=True) * (1.0 / D)
        cubed = inverse * inverse * inverse * dot
        for at in range(0, D, width):
            columns = pl.ds(at, width)
            values = hidden_ref[0, rows, columns].astype(F32)
            out[rows, columns] = (inverse * gained[:, columns] - values * cubed).astype(BF16)
        copy = pltpu.make_async_copy(out.at[rows], out_hbm.at[0, rows], sems.at[start // BLOCK])
        copy.start()
        copies.append(copy)
    for copy in copies:
        copy.wait()


def local(hidden, segment_ids, assign, positive, gain):
    shape = jax.ShapeDtypeStruct
    gain = gain.reshape(1, D)
    with jax.named_scope("pool"):
        send, upright, partner = pl.pallas_call(
            pool_kernel,
            out_shape=(
                shape((2, N_ZL, 8, QUARTER + META), BF16),
                shape((ROWS, 128), F32),
                shape((1, BATCH), jnp.int32),
            ),
            in_specs=[HBM] * 5,
            out_specs=(VMEM, VMEM, VMEM),
            scratch_shapes=[
                pltpu.VMEM((ROWS, D), BF16),
                pltpu.VMEM((1, 1, ROWS), jnp.int32),
                pltpu.VMEM((1, PAS), jnp.int32),
                pltpu.VMEM((1, D), F32),
                pltpu.VMEM((PAS, 64), jnp.int32),
                pltpu.SemaphoreType.DMA((D // CHUNK,)),
                pltpu.SemaphoreType.DMA((4,)),
            ],
            compiler_params=PARAMS,
        )(*[pltpu.with_memory_space_constraint(v, pltpu.HBM) for v in (hidden, segment_ids, assign, gain, positive.T)])
    with jax.named_scope("pooled_to_relay"):
        pooled = lax.all_to_all(send.reshape(2 * N_ZL, 8, -1), ("core", "zl"), 0, 0)
        pooled = pooled.reshape(2 * N_ZL * 8, -1)
    with jax.named_scope("relay"):
        send, back = pl.pallas_call(
            relay_kernel,
            out_shape=(shape((N_ZH, 8, HALF), BF16), shape((128, META), F32)),
            in_specs=[VMEM],
            out_specs=(VMEM, VMEM),
            compiler_params=PARAMS,
        )(pooled)
    with jax.named_scope("pooled_to_owner"):
        pooled = lax.all_to_all(send, "zh", 0, 0)
    with jax.named_scope("owned"):
        send, embed = pl.pallas_call(
            owned_kernel,
            out_shape=(shape((N_Y, 8, HALF), BF16), shape((8, HALF), F32)),
            in_specs=[VMEM],
            out_specs=(VMEM, VMEM),
            compiler_params=PARAMS,
        )(pooled)
    with jax.named_scope("embed_exchange"):
        batch = lax.all_to_all(send, "y", 0, 0).reshape(N_Y * 8, HALF)
        batch = jnp.broadcast_to(batch, (N_X, N_Y * 8, HALF))
        batch = lax.all_to_all(batch, "x", 0, 0).reshape(BATCH, HALF)
    with jax.named_scope("gram"):
        gram = pl.pallas_call(
            gram_kernel,
            out_shape=shape((BATCH, BATCH), F32),
            in_specs=[VMEM],
            out_specs=VMEM,
            compiler_params=PARAMS,
        )(batch)
        gram = lax.all_gather(gram, "core", axis=0)
    with jax.named_scope("contrast"):
        loss, send = pl.pallas_call(
            contrast_kernel,
            out_shape=(shape((1, PAS), F32), shape((N_ZH, 8, HALF), BF16)),
            in_specs=[VMEM] * 4,
            out_specs=(VMEM, VMEM),
            compiler_params=PARAMS,
        )(gram, batch, embed, partner)
    with jax.named_scope("grad_to_relay"):
        grads = lax.all_to_all(send, "zh", 0, 0).reshape(N_ZH * 8, HALF)
    with jax.named_scope("back"):
        send = pl.pallas_call(
            back_kernel,
            out_shape=shape((2, N_ZL, 8, QUARTER), BF16),
            in_specs=[VMEM, VMEM],
            out_specs=VMEM,
            compiler_params=PARAMS,
        )(grads, back)
    with jax.named_scope("grad_to_rows"):
        grads = lax.all_to_all(send.reshape(2 * N_ZL, 8, QUARTER), ("core", "zl"), 0, 0)
        grads = grads.reshape(2, N_ZL, 8, QUARTER)
    with jax.named_scope("rows"):
        grad_rows = pl.pallas_call(
            rows_kernel,
            out_shape=shape((1, ROWS, D), BF16),
            in_specs=[VMEM] * 5,
            out_specs=HBM,
            scratch_shapes=[
                pltpu.VMEM((24, D), BF16),
                pltpu.VMEM((BLOCK, D), F32),
                pltpu.VMEM((ROWS, D), BF16),
                pltpu.SemaphoreType.DMA((ROWS // BLOCK,)),
            ],
            compiler_params=PARAMS,
        )(grads, hidden, segment_ids, gain, upright)
    return loss, grad_rows


def solution(mesh):
    fine = Mesh(
        mesh.devices.reshape(N_X, N_Y, 2, N_ZH, N_ZL), ("x", "y", "core", "zh", "zl")
    )
    group, dp = ("x", "y", "core"), ("zh", "zl")
    placed = (P(group, dp, None), P(group, dp, None), P(group, dp), P(None, dp), P())
    return jax.shard_map(
        local,
        mesh=fine,
        in_specs=placed,
        out_specs=(P(group, dp), P(group, dp, None)),
        check_vma=False,
    )
```

```python
import functools

import jax
import jax.numpy as jnp
from jax import lax
from jax.experimental import pallas as pl
from jax.experimental.pallas import tpu as pltpu
from jax.sharding import Mesh
from jax.sharding import PartitionSpec as P

inv_tau = 20.0
loss_scale = 1024.0
norm_eps = 1e-06

F32 = jnp.float32
BF16 = jnp.bfloat16
ROWS = 256
D = 4096
HALF = D // 2
QUARTER = D // 4
PAS = 4
CHUNK = 1024
BLOCK = 64
META = 128
N_ZH = 3
N_ZL = 4
N_X = 4
N_Y = 8
BATCH = 256

VMEM = pl.BlockSpec(memory_space=pltpu.VMEM)
HBM = pl.BlockSpec(memory_space=pltpu.HBM)
PARAMS = pltpu.CompilerParams(vmem_limit_bytes=40 * 1024 * 1024)


def iota(shape, dim):
    return lax.broadcasted_iota(jnp.int32, shape, dim)


def split3(values):
    high = values.astype(BF16).astype(F32)
    rest = values - high
    middle = rest.astype(BF16).astype(F32)
    low = rest - middle
    return jnp.concatenate([high, middle, low], axis=0).astype(BF16)


def sum3(values):
    return values[0:8] + values[8:16] + values[16:24]


def pool_kernel(
    hidden_hbm, segment_hbm, assign_hbm, gain_hbm, positive_hbm,
    send_ref, upright_ref, partner_ref,
    hidden, segment_at, assign_at, gain, positive, chunk_sem, small_sem,
):
    chunks = [pl.ds(at * CHUNK, CHUNK) for at in range(D // CHUNK)]
    copies = [
        pltpu.make_async_copy(hidden_hbm.at[0, :, part], hidden.at[:, part], chunk_sem.at[at])
        for at, part in enumerate(chunks)
    ]
    small = [
        pltpu.make_async_copy(source, target, small_sem.at[at])
        for at, (source, target) in enumerate(
            [(segment_hbm, segment_at), (assign_hbm, assign_at), (positive_hbm, positive), (gain_hbm, gain)]
        )
    ]
    copies[0].start()
    for copy in small:
        copy.start()
    for copy in copies[1:]:
        copy.start()

    for copy in small:
        copy.wait()
    segment = jnp.broadcast_to(segment_at[0], (8, ROWS))
    onehot = jnp.where(segment == iota((8, ROWS), 0), 1.0, 0.0)
    counts = jnp.maximum(jnp.sum(onehot, axis=1, keepdims=True), 1.0)
    row = iota((8, META), 0)
    owner = jnp.zeros((8, META), jnp.int32)
    for k in range(PAS):
        owner = jnp.where(lax.rem(row, PAS) == k, assign_at[0:1, k : k + 1], owner)
    place = lax.axis_index("core") * 32 + lax.axis_index("zl") * 8 + row
    meta = jnp.where(iota((8, META), 1) == place, owner, 0).astype(F32).astype(BF16)
    for h in range(2):
        for peer in range(N_ZL):
            send_ref[h, peer, :, QUARTER:] = meta
    lane = iota((64, BATCH), 1)
    spread = jnp.where(lax.div(lane, PAS) == iota((64, BATCH), 0), 1.0, 0.0).astype(BF16)
    partner = jnp.concatenate([positive[...].astype(F32), jnp.zeros((PAS, 64), F32)], axis=0)
    partner = jnp.dot(partner.astype(BF16), spread, preferred_element_type=F32)
    partner = jnp.where(lax.rem(iota((8, BATCH), 1), PAS) == iota((8, BATCH), 0), partner, 0.0)
    partner_ref[...] = jnp.sum(partner, axis=0, keepdims=True).astype(jnp.int32)

    total = jnp.zeros((ROWS, 128), F32)
    for at, part in enumerate(chunks):
        copies[at].wait()
        for piece in range(0, CHUNK, 128):
            values = hidden[:, at * CHUNK + piece : at * CHUNK + piece + 128].astype(F32)
            total = total + values * values
    squares = jnp.sum(total.T, axis=0, keepdims=True)
    inverse = jnp.broadcast_to(lax.rsqrt(squares * (1.0 / D) + norm_eps), (8, ROWS))
    weights = split3(onehot * inverse)
    for h in range(2):
        columns = pl.ds(h * HALF, HALF)
        pooled = sum3(jnp.dot(weights, hidden[:, columns], preferred_element_type=F32))
        pooled = (pooled * gain[:, columns] / counts)[0:PAS]
        pooled = jnp.concatenate([pooled[:, 0:QUARTER], pooled[:, QUARTER:]], axis=0).astype(BF16)
        for peer in range(N_ZL):
            send_ref[h, peer, :, 0:QUARTER] = pooled
    upright_ref[...] = jnp.concatenate(
        [onehot, onehot, onehot, inverse, jnp.zeros((96, ROWS), F32)], axis=0
    ).T


def relay_kernel(pooled_ref, send_ref, back_ref):
    relay = lax.axis_index("zl")
    owners = jnp.sum(pooled_ref[:, QUARTER:].astype(F32), axis=0, keepdims=True)
    row = iota((128, META), 0)
    lane = iota((128, META), 1)
    slot = (lax.div(row, 8) * N_ZL + relay) * PAS + lax.rem(row, PAS)
    hit = (owners == slot.astype(F32)) & (lax.div(lane, 32) == lax.div(lax.rem(row, 8), PAS))
    hit = hit & (row < N_ZH * 8) & (lane < 64)
    select = jnp.where(hit, 1.0, 0.0)
    back_ref[...] = select.T
    pooled = pooled_ref[:, 0:QUARTER]
    for q in range(2):
        part = jnp.where(lax.rem(lax.div(lane, PAS), 2) == q, select, 0.0)[0 : N_ZH * 8, 0:64]
        kept = jnp.dot(part.astype(BF16), pooled, preferred_element_type=F32)
        for peer in range(N_ZH):
            send_ref[peer, :, q * QUARTER : (q + 1) * QUARTER] = kept[
                peer * 8 : (peer + 1) * 8
            ].astype(BF16)


def owned_kernel(pooled_ref, send_ref, embed_ref):
    own = pooled_ref[0].astype(F32)
    for peer in range(1, N_ZH):
        own = own + pooled_ref[peer].astype(F32)
    embed_ref[...] = own
    send_ref[...] = own.astype(BF16)


def gram_kernel(embed_ref, gram_ref):
    embeds = embed_ref[...]
    gram_ref[...] = lax.dot_general(
        embeds, embeds, (((1,), (1,)), ((), ())), preferred_element_type=F32
    )


def contrast_kernel(gram_ref, batch_ref, embed_ref, partner_ref, loss_ref, send_ref):
    core = lax.axis_index("core")
    first = (lax.axis_index("x") * 8 + lax.axis_index("y")) * 8
    shift = inv_tau
    row = iota((8, BATCH), 0)
    lane = iota((8, BATCH), 1)
    mine = first + row
    partner = partner_ref[...]
    own_partner = jnp.sum(jnp.where(lane == mine, partner, 0), axis=1, keepdims=True)

    gram = gram_ref[0] + gram_ref[1]
    everyone = iota((BATCH, BATCH), 0) == iota((BATCH, BATCH), 1)
    diagonal = jnp.where(everyone, gram, 0.0)
    across = lax.rsqrt(jnp.sum(diagonal, axis=0, keepdims=True) + norm_eps)
    down = lax.rsqrt(jnp.sum(diagonal, axis=1, keepdims=True) + norm_eps)
    logits = jnp.where(everyone, -1e30, gram * down * across * inv_tau)
    lse_all = shift + jnp.log(jnp.sum(jnp.exp(logits - shift), axis=0, keepdims=True))
    at = pl.ds(pl.multiple_of(first, 8), 8)
    own = gram_ref[0, at, :] + gram_ref[1, at, :]
    scale = lax.rsqrt(
        jnp.sum(jnp.where(lane == mine, own, 0.0), axis=1, keepdims=True) + norm_eps
    )
    cosine = own * scale * across
    own = jnp.where(lane == mine, -1e30, cosine * inv_tau)
    lse = shift + jnp.log(jnp.sum(jnp.exp(own - shift), axis=1, keepdims=True))
    hits = lane == own_partner
    loss = lse - jnp.sum(jnp.where(hits, own, 0.0), axis=1, keepdims=True)
    as_query = loss_scale * (jnp.exp(own - lse) - jnp.where(hits, 1.0, 0.0))
    as_key = loss_scale * (jnp.exp(own - lse_all) - jnp.where(partner == mine, 1.0, 0.0))
    weights = as_query.astype(BF16).astype(F32) + as_key.astype(BF16).astype(F32)
    inner = inv_tau * jnp.sum(weights * cosine, axis=1, keepdims=True)
    pair = jnp.concatenate([as_query, as_key], axis=0).astype(BF16)
    width = 512
    for start in range(0, HALF, width):
        columns = pl.ds(start, width)
        units = (batch_ref[:, columns].astype(F32) * down).astype(BF16)
        grad = jnp.dot(pair, units, preferred_element_type=F32)
        grad = (grad[0:8] + grad[8:16]) * inv_tau - embed_ref[:, columns] * (scale * inner)
        grad = (grad * scale).astype(BF16)
        for peer in range(N_ZH):
            send_ref[peer, :, columns] = grad
    place = (iota((8, 128), 1) + core * PAS) == iota((8, 128), 0)
    loss = jnp.sum(jnp.where(place, loss, 0.0), axis=0, keepdims=True)
    loss_ref[...] = loss[:, 0:PAS]


def back_kernel(grad_ref, back_ref, send_ref):
    back = back_ref[...]
    row = iota((128, META), 0)
    total = jnp.zeros((64, QUARTER), F32)
    for q in range(2):
        part = jnp.where(lax.rem(lax.div(row, PAS), 2) == q, back, 0.0)[0:64, 0 : N_ZH * 8]
        total = total + jnp.dot(
            part.astype(BF16),
            grad_ref[:, q * QUARTER : (q + 1) * QUARTER],
            preferred_element_type=F32,
        )
    total = total.astype(BF16)
    for c in range(2):
        for peer in range(N_ZL):
            at = (c * N_ZL + peer) * 8
            send_ref[c, peer] = total[at : at + 8]


def rows_kernel(
    grad_ref, hidden_ref, segment_ref, gain_ref, upright_ref, out_hbm,
    scaled, gained, out, sems,
):
    segment = jnp.broadcast_to(segment_ref[0], (8, ROWS))
    onehot = jnp.where(segment == iota((8, ROWS), 0), 1.0, 0.0)
    counts = jnp.maximum(jnp.sum(onehot, axis=1, keepdims=True), 1.0)
    for h in range(2):
        part = grad_ref[h, 0].astype(F32)
        for peer in range(1, N_ZL):
            part = part + grad_ref[h, peer].astype(F32)
        for q in range(2):
            columns = pl.ds((h * 2 + q) * QUARTER, QUARTER)
            scaled[:, columns] = split3(gain_ref[:, columns] * (part / counts))
            part = jnp.concatenate([part[PAS:], part[0:PAS]], axis=0)
    width = 1024
    copies = []
    for start in range(0, ROWS, BLOCK):
        rows = pl.ds(start, BLOCK)
        spread = upright_ref[rows, 0:24].astype(BF16)
        inverse = upright_ref[rows, 24:25]
        total = jnp.zeros((BLOCK, 128), F32)
        for at in range(0, D, width):
            columns = pl.ds(at, width)
            part = jnp.dot(spread, scaled[:, columns], preferred_element_type=F32)
            gained[:, columns] = part
            part = part * hidden_ref[0, rows, columns].astype(F32)
            for piece in range(0, width, 128):
                total = total + part[:, piece : piece + 128]
        dot = jnp.sum(total, axis=1, keepdims=True) * (1.0 / D)
        cubed = inverse * inverse * inverse * dot
        for at in range(0, D, width):
            columns = pl.ds(at, width)
            values = hidden_ref[0, rows, columns].astype(F32)
            out[rows, columns] = (inverse * gained[:, columns] - values * cubed).astype(BF16)
        copy = pltpu.make_async_copy(out.at[rows], out_hbm.at[0, rows], sems.at[start // BLOCK])
        copy.start()
        copies.append(copy)
    for copy in copies:
        copy.wait()


def gather(block, axis, size):
    return lax.all_to_all(jnp.broadcast_to(block, (size,) + block.shape), axis, 0, 0)


def along_y_x(block):
    column = gather(block, "y", N_Y).reshape(N_Y * 8, HALF)
    return gather(column, "x", N_X).reshape(BATCH, HALF)


def along_x_y(block):
    line = gather(block, "x", N_X).reshape(N_X * 8, HALF)
    batch = gather(line, "y", N_Y).reshape(N_Y, N_X, 8, HALF)
    return batch.transpose(1, 0, 2, 3).reshape(BATCH, HALF)


def local(hidden, segment_ids, assign, positive, gain):
    shape = jax.ShapeDtypeStruct
    gain = gain.reshape(1, D)
    with jax.named_scope("pool"):
        send, upright, partner = pl.pallas_call(
            pool_kernel,
            out_shape=(
                shape((2, N_ZL, 8, QUARTER + META), BF16),
                shape((ROWS, 128), F32),
                shape((1, BATCH), jnp.int32),
            ),
            in_specs=[HBM] * 5,
            out_specs=(VMEM, VMEM, VMEM),
            scratch_shapes=[
                pltpu.VMEM((ROWS, D), BF16),
                pltpu.VMEM((1, 1, ROWS), jnp.int32),
                pltpu.VMEM((1, PAS), jnp.int32),
                pltpu.VMEM((1, D), F32),
                pltpu.VMEM((PAS, 64), jnp.int32),
                pltpu.SemaphoreType.DMA((D // CHUNK,)),
                pltpu.SemaphoreType.DMA((4,)),
            ],
            compiler_params=PARAMS,
        )(*[pltpu.with_memory_space_constraint(v, pltpu.HBM) for v in (hidden, segment_ids, assign, gain, positive.T)])
    with jax.named_scope("pooled_to_relay"):
        send, core = lax.optimization_barrier((send, lax.axis_index("core")))
        pooled = lax.all_to_all(send.reshape(2 * N_ZL, 8, -1), ("core", "zl"), 0, 0)
        pooled = pooled.reshape(2 * N_ZL * 8, -1)
    with jax.named_scope("relay"):
        send, back = pl.pallas_call(
            relay_kernel,
            out_shape=(shape((N_ZH, 8, HALF), BF16), shape((128, META), F32)),
            in_specs=[VMEM],
            out_specs=(VMEM, VMEM),
            compiler_params=PARAMS,
        )(pooled)
    with jax.named_scope("pooled_to_owner"):
        pooled = lax.all_to_all(send, "zh", 0, 0)
    with jax.named_scope("owned"):
        send, embed = pl.pallas_call(
            owned_kernel,
            out_shape=(shape((8, HALF), BF16), shape((8, HALF), F32)),
            in_specs=[VMEM],
            out_specs=(VMEM, VMEM),
            compiler_params=PARAMS,
        )(pooled)
    with jax.named_scope("embed_exchange"):
        send, core = lax.optimization_barrier((send, core))
        batch = lax.cond(core == 0, along_y_x, along_x_y, send)
    with jax.named_scope("gram"):
        gram = pl.pallas_call(
            gram_kernel,
            out_shape=shape((BATCH, BATCH), F32),
            in_specs=[VMEM],
            out_specs=VMEM,
            compiler_params=PARAMS,
        )(batch)
        gram = lax.all_gather(gram, "core", axis=0)
    with jax.named_scope("contrast"):
        loss, send = pl.pallas_call(
            contrast_kernel,
            out_shape=(shape((1, PAS), F32), shape((N_ZH, 8, HALF), BF16)),
            in_specs=[VMEM] * 4,
            out_specs=(VMEM, VMEM),
            compiler_params=PARAMS,
        )(gram, batch, embed, partner)
    with jax.named_scope("grad_to_relay"):
        grads = lax.all_to_all(send, "zh", 0, 0).reshape(N_ZH * 8, HALF)
    with jax.named_scope("back"):
        send = pl.pallas_call(
            back_kernel,
            out_shape=shape((2, N_ZL, 8, QUARTER), BF16),
            in_specs=[VMEM, VMEM],
            out_specs=VMEM,
            compiler_params=PARAMS,
        )(grads, back)
    with jax.named_scope("grad_to_rows"):
        grads = lax.all_to_all(send.reshape(2 * N_ZL, 8, QUARTER), ("core", "zl"), 0, 0)
        grads = grads.reshape(2, N_ZL, 8, QUARTER)
    with jax.named_scope("rows"):
        grad_rows = pl.pallas_call(
            rows_kernel,
            out_shape=shape((1, ROWS, D), BF16),
            in_specs=[VMEM] * 5,
            out_specs=HBM,
            scratch_shapes=[
                pltpu.VMEM((24, D), BF16),
                pltpu.VMEM((BLOCK, D), F32),
                pltpu.VMEM((ROWS, D), BF16),
                pltpu.SemaphoreType.DMA((ROWS // BLOCK,)),
            ],
            compiler_params=PARAMS,
        )(grads, hidden, segment_ids, gain, upright)
    return loss, grad_rows


def solution(mesh):
    fine = Mesh(
        mesh.devices.reshape(N_X, N_Y, 2, N_ZH, N_ZL), ("x", "y", "core", "zh", "zl")
    )
    group, dp = ("x", "y", "core"), ("zh", "zl")
    placed = (P(group, dp, None), P(group, dp, None), P(group, dp), P(None, dp), P())
    return jax.shard_map(
        local,
        mesh=fine,
        in_specs=placed,
        out_specs=(P(group, dp), P(group, dp, None)),
        check_vma=False,
    )
```

```python
import functools

import jax
import jax.numpy as jnp
from jax import lax
from jax.experimental import pallas as pl
from jax.experimental.pallas import tpu as pltpu
from jax.sharding import Mesh
from jax.sharding import PartitionSpec as P

inv_tau = 20.0
loss_scale = 1024.0
norm_eps = 1e-06

F32 = jnp.float32
BF16 = jnp.bfloat16
ROWS = 256
D = 4096
HALF = D // 2
QUARTER = D // 4
PAS = 4
CHUNK = 2048
BLOCK = 64
META = 128
N_ZH = 3
N_ZL = 4
N_X = 4
N_Y = 8
BATCH = 256

VMEM = pl.BlockSpec(memory_space=pltpu.VMEM)
HBM = pl.BlockSpec(memory_space=pltpu.HBM)
PARAMS = pltpu.CompilerParams(vmem_limit_bytes=40 * 1024 * 1024)


def iota(shape, dim):
    return lax.broadcasted_iota(jnp.int32, shape, dim)


def split3(values):
    high = values.astype(BF16).astype(F32)
    rest = values - high
    middle = rest.astype(BF16).astype(F32)
    low = rest - middle
    return jnp.concatenate([high, middle, low], axis=0).astype(BF16)


def sum3(values):
    return values[0:8] + values[8:16] + values[16:24]


def pool_kernel(
    hidden_hbm, segment_hbm, assign_hbm, gain_hbm, positive_hbm,
    send_ref, upright_ref, partner_ref,
    hidden, segment_at, assign_at, gain, positive, chunk_sem, small_sem,
):
    chunks = [pl.ds(at * CHUNK, CHUNK) for at in range(D // CHUNK)]
    copies = [
        pltpu.make_async_copy(hidden_hbm.at[0, :, part], hidden.at[:, part], chunk_sem.at[at])
        for at, part in enumerate(chunks)
    ]
    small = [
        pltpu.make_async_copy(source, target, small_sem.at[at])
        for at, (source, target) in enumerate(
            [(segment_hbm, segment_at), (assign_hbm, assign_at), (positive_hbm, positive), (gain_hbm, gain)]
        )
    ]
    copies[0].start()
    for copy in small:
        copy.start()
    for copy in copies[1:]:
        copy.start()

    for copy in small:
        copy.wait()
    segment = jnp.broadcast_to(segment_at[0], (8, ROWS))
    onehot = jnp.where(segment == iota((8, ROWS), 0), 1.0, 0.0)
    counts = jnp.maximum(jnp.sum(onehot, axis=1, keepdims=True), 1.0)
    row = iota((8, META), 0)
    owner = jnp.zeros((8, META), jnp.int32)
    for k in range(PAS):
        owner = jnp.where(lax.rem(row, PAS) == k, assign_at[0:1, k : k + 1], owner)
    place = lax.axis_index("zl") * 16 + lax.axis_index("core") * 8 + row
    meta = jnp.where(iota((8, META), 1) == place, owner, 0).astype(F32).astype(BF16)
    for h in range(2):
        for peer in range(N_ZL):
            send_ref[peer, h, :, QUARTER:] = meta
    lane = iota((64, BATCH), 1)
    spread = jnp.where(lax.div(lane, PAS) == iota((64, BATCH), 0), 1.0, 0.0).astype(BF16)
    partner = jnp.concatenate([positive[...].astype(F32), jnp.zeros((PAS, 64), F32)], axis=0)
    partner = jnp.dot(partner.astype(BF16), spread, preferred_element_type=F32)
    partner = jnp.where(lax.rem(iota((8, BATCH), 1), PAS) == iota((8, BATCH), 0), partner, 0.0)
    partner_ref[...] = jnp.sum(partner, axis=0, keepdims=True).astype(jnp.int32)

    total = jnp.zeros((ROWS, 128), F32)
    for at, part in enumerate(chunks):
        copies[at].wait()
        for piece in range(0, CHUNK, 128):
            values = hidden[:, at * CHUNK + piece : at * CHUNK + piece + 128].astype(F32)
            total = total + values * values
    squares = jnp.sum(total.T, axis=0, keepdims=True)
    inverse = jnp.broadcast_to(lax.rsqrt(squares * (1.0 / D) + norm_eps), (8, ROWS))
    weights = split3(onehot * inverse)
    for h in range(2):
        columns = pl.ds(h * HALF, HALF)
        pooled = sum3(jnp.dot(weights, hidden[:, columns], preferred_element_type=F32))
        pooled = (pooled * gain[:, columns] / counts)[0:PAS]
        pooled = jnp.concatenate([pooled[:, 0:QUARTER], pooled[:, QUARTER:]], axis=0).astype(BF16)
        for peer in range(N_ZL):
            send_ref[peer, h, :, 0:QUARTER] = pooled
    upright_ref[...] = jnp.concatenate(
        [onehot, onehot, onehot, inverse, jnp.zeros((96, ROWS), F32)], axis=0
    ).T


def relay_kernel(pooled_ref, send_ref, back_ref):
    relay = lax.axis_index("zl")
    owners = jnp.sum(pooled_ref[:, QUARTER:].astype(F32), axis=0, keepdims=True)
    row = iota((128, META), 0)
    lane = iota((128, META), 1)
    slot = (lax.div(row, 8) * N_ZL + relay) * PAS + lax.rem(row, PAS)
    hit = (owners == slot.astype(F32)) & (lax.rem(lax.div(lane, 8), 2) == lax.div(lax.rem(row, 8), PAS))
    hit = hit & (row < N_ZH * 8) & (lane < 64)
    select = jnp.where(hit, 1.0, 0.0)
    back_ref[...] = select.T
    pooled = pooled_ref[:, 0:QUARTER]
    for q in range(2):
        part = jnp.where(lax.rem(lax.div(lane, PAS), 2) == q, select, 0.0)[0 : N_ZH * 8, 0:64]
        kept = jnp.dot(part.astype(BF16), pooled, preferred_element_type=F32)
        for peer in range(N_ZH):
            send_ref[peer, :, q * QUARTER : (q + 1) * QUARTER] = kept[
                peer * 8 : (peer + 1) * 8
            ].astype(BF16)


def owned_kernel(pooled_ref, send_ref, embed_ref):
    own = pooled_ref[0].astype(F32)
    for peer in range(1, N_ZH):
        own = own + pooled_ref[peer].astype(F32)
    embed_ref[...] = own
    send_ref[...] = own.astype(BF16)


def gram_kernel(embed_ref, gram_ref):
    embeds = embed_ref[...]
    gram_ref[...] = lax.dot_general(
        embeds, embeds, (((1,), (1,)), ((), ())), preferred_element_type=F32
    )


def contrast_kernel(gram_ref, batch_ref, embed_ref, partner_ref, loss_ref, send_ref):
    core = lax.axis_index("core")
    first = (lax.axis_index("x") * 8 + lax.axis_index("y")) * 8
    shift = inv_tau
    row = iota((8, BATCH), 0)
    lane = iota((8, BATCH), 1)
    mine = first + row
    partner = partner_ref[...]
    own_partner = jnp.sum(jnp.where(lane == mine, partner, 0), axis=1, keepdims=True)

    gram = gram_ref[0] + gram_ref[1]
    everyone = iota((BATCH, BATCH), 0) == iota((BATCH, BATCH), 1)
    diagonal = jnp.where(everyone, gram, 0.0)
    across = lax.rsqrt(jnp.sum(diagonal, axis=0, keepdims=True) + norm_eps)
    down = lax.rsqrt(jnp.sum(diagonal, axis=1, keepdims=True) + norm_eps)
    logits = jnp.where(everyone, -1e30, gram * down * across * inv_tau)
    lse_all = shift + jnp.log(jnp.sum(jnp.exp(logits - shift), axis=0, keepdims=True))
    at = pl.ds(pl.multiple_of(first, 8), 8)
    own = gram_ref[0, at, :] + gram_ref[1, at, :]
    scale = lax.rsqrt(
        jnp.sum(jnp.where(lane == mine, own, 0.0), axis=1, keepdims=True) + norm_eps
    )
    cosine = own * scale * across
    own = jnp.where(lane == mine, -1e30, cosine * inv_tau)
    lse = shift + jnp.log(jnp.sum(jnp.exp(own - shift), axis=1, keepdims=True))
    hits = lane == own_partner
    loss = lse - jnp.sum(jnp.where(hits, own, 0.0), axis=1, keepdims=True)
    as_query = loss_scale * (jnp.exp(own - lse) - jnp.where(hits, 1.0, 0.0))
    as_key = loss_scale * (jnp.exp(own - lse_all) - jnp.where(partner == mine, 1.0, 0.0))
    weights = as_query.astype(BF16).astype(F32) + as_key.astype(BF16).astype(F32)
    inner = inv_tau * jnp.sum(weights * cosine, axis=1, keepdims=True)
    pair = jnp.concatenate([as_query, as_key], axis=0).astype(BF16)
    width = 512
    for start in range(0, HALF, width):
        columns = pl.ds(start, width)
        units = (batch_ref[:, columns].astype(F32) * down).astype(BF16)
        grad = jnp.dot(pair, units, preferred_element_type=F32)
        grad = (grad[0:8] + grad[8:16]) * inv_tau - embed_ref[:, columns] * (scale * inner)
        grad = (grad * scale).astype(BF16)
        for peer in range(N_ZH):
            send_ref[peer, :, columns] = grad
    place = (iota((8, 128), 1) + core * PAS) == iota((8, 128), 0)
    loss = jnp.sum(jnp.where(place, loss, 0.0), axis=0, keepdims=True)
    loss_ref[...] = loss[:, 0:PAS]


def back_kernel(grad_ref, back_ref, send_ref):
    back = back_ref[...]
    row = iota((128, META), 0)
    total = jnp.zeros((64, QUARTER), F32)
    for q in range(2):
        part = jnp.where(lax.rem(lax.div(row, PAS), 2) == q, back, 0.0)[0:64, 0 : N_ZH * 8]
        total = total + jnp.dot(
            part.astype(BF16),
            grad_ref[:, q * QUARTER : (q + 1) * QUARTER],
            preferred_element_type=F32,
        )
    total = total.astype(BF16)
    for peer in range(N_ZL):
        for c in range(2):
            at = (peer * 2 + c) * 8
            send_ref[peer, c] = total[at : at + 8]


def rows_kernel(
    grad_ref, hidden_ref, segment_ref, gain_ref, upright_ref, out_hbm,
    scaled, gained, out, sems,
):
    segment = jnp.broadcast_to(segment_ref[0], (8, ROWS))
    onehot = jnp.where(segment == iota((8, ROWS), 0), 1.0, 0.0)
    counts = jnp.maximum(jnp.sum(onehot, axis=1, keepdims=True), 1.0)
    for h in range(2):
        part = grad_ref[0, h].astype(F32)
        for peer in range(1, N_ZL):
            part = part + grad_ref[peer, h].astype(F32)
        for q in range(2):
            columns = pl.ds((h * 2 + q) * QUARTER, QUARTER)
            scaled[:, columns] = split3(gain_ref[:, columns] * (part / counts))
            part = jnp.concatenate([part[PAS:], part[0:PAS]], axis=0)
    width = 1024
    copies = []
    for start in range(0, ROWS, BLOCK):
        rows = pl.ds(start, BLOCK)
        spread = upright_ref[rows, 0:24].astype(BF16)
        inverse = upright_ref[rows, 24:25]
        total = jnp.zeros((BLOCK, 128), F32)
        for at in range(0, D, width):
            columns = pl.ds(at, width)
            part = jnp.dot(spread, scaled[:, columns], preferred_element_type=F32)
            gained[:, columns] = part
            part = part * hidden_ref[0, rows, columns].astype(F32)
            for piece in range(0, width, 128):
                total = total + part[:, piece : piece + 128]
        dot = jnp.sum(total, axis=1, keepdims=True) * (1.0 / D)
        cubed = inverse * inverse * inverse * dot
        for at in range(0, D, width):
            columns = pl.ds(at, width)
            values = hidden_ref[0, rows, columns].astype(F32)
            out[rows, columns] = (inverse * gained[:, columns] - values * cubed).astype(BF16)
        copy = pltpu.make_async_copy(out.at[rows], out_hbm.at[0, rows], sems.at[start // BLOCK])
        copy.start()
        copies.append(copy)
    for copy in copies:
        copy.wait()


def gather(block, axis, size):
    return lax.all_to_all(jnp.broadcast_to(block, (size,) + block.shape), axis, 0, 0)


def along_y_x(block):
    column = gather(block, "y", N_Y).reshape(N_Y * 8, HALF)
    return gather(column, "x", N_X).reshape(BATCH, HALF)


def along_x_y(block):
    line = gather(block, "x", N_X).reshape(N_X * 8, HALF)
    batch = gather(line, "y", N_Y).reshape(N_Y, N_X, 8, HALF)
    return batch.transpose(1, 0, 2, 3).reshape(BATCH, HALF)


def local(hidden, segment_ids, assign, positive, gain):
    shape = jax.ShapeDtypeStruct
    gain = gain.reshape(1, D)
    with jax.named_scope("pool"):
        send, upright, partner = pl.pallas_call(
            pool_kernel,
            out_shape=(
                shape((N_ZL, 2, 8, QUARTER + META), BF16),
                shape((ROWS, 128), F32),
                shape((1, BATCH), jnp.int32),
            ),
            in_specs=[HBM] * 5,
            out_specs=(VMEM, VMEM, VMEM),
            scratch_shapes=[
                pltpu.VMEM((ROWS, D), BF16),
                pltpu.VMEM((1, 1, ROWS), jnp.int32),
                pltpu.VMEM((1, PAS), jnp.int32),
                pltpu.VMEM((1, D), F32),
                pltpu.VMEM((PAS, 64), jnp.int32),
                pltpu.SemaphoreType.DMA((D // CHUNK,)),
                pltpu.SemaphoreType.DMA((4,)),
            ],
            compiler_params=PARAMS,
        )(*[pltpu.with_memory_space_constraint(v, pltpu.HBM) for v in (hidden, segment_ids, assign, gain, positive.T)])
    with jax.named_scope("pooled_to_relay"):
        send, core = lax.optimization_barrier((send, lax.axis_index("core")))
        pooled = lax.all_to_all(send.reshape(N_ZL * 2, 8, -1), ("zl", "core"), 0, 0)
        pooled = pooled.reshape(N_ZL * 2 * 8, -1)
    with jax.named_scope("relay"):
        send, back = pl.pallas_call(
            relay_kernel,
            out_shape=(shape((N_ZH, 8, HALF), BF16), shape((128, META), F32)),
            in_specs=[VMEM],
            out_specs=(VMEM, VMEM),
            compiler_params=PARAMS,
        )(pooled)
    with jax.named_scope("pooled_to_owner"):
        pooled = lax.all_to_all(send, "zh", 0, 0)
    with jax.named_scope("owned"):
        send, embed = pl.pallas_call(
            owned_kernel,
            out_shape=(shape((8, HALF), BF16), shape((8, HALF), F32)),
            in_specs=[VMEM],
            out_specs=(VMEM, VMEM),
            compiler_params=PARAMS,
        )(pooled)
    with jax.named_scope("embed_exchange"):
        send, core = lax.optimization_barrier((send, core))
        batch = lax.cond(core == 0, along_y_x, along_x_y, send)
    with jax.named_scope("gram"):
        gram = pl.pallas_call(
            gram_kernel,
            out_shape=shape((BATCH, BATCH), F32),
            in_specs=[VMEM],
            out_specs=VMEM,
            compiler_params=PARAMS,
        )(batch)
        gram = lax.all_gather(gram, "core", axis=0)
    with jax.named_scope("contrast"):
        loss, send = pl.pallas_call(
            contrast_kernel,
            out_shape=(shape((1, PAS), F32), shape((N_ZH, 8, HALF), BF16)),
            in_specs=[VMEM] * 4,
            out_specs=(VMEM, VMEM),
            compiler_params=PARAMS,
        )(gram, batch, embed, partner)
    with jax.named_scope("grad_to_relay"):
        grads = lax.all_to_all(send, "zh", 0, 0).reshape(N_ZH * 8, HALF)
    with jax.named_scope("back"):
        send = pl.pallas_call(
            back_kernel,
            out_shape=shape((N_ZL, 2, 8, QUARTER), BF16),
            in_specs=[VMEM, VMEM],
            out_specs=VMEM,
            compiler_params=PARAMS,
        )(grads, back)
    with jax.named_scope("grad_to_rows"):
        grads = lax.all_to_all(send.reshape(N_ZL * 2, 8, QUARTER), ("zl", "core"), 0, 0)
        grads = grads.reshape(N_ZL, 2, 8, QUARTER)
    with jax.named_scope("rows"):
        grad_rows = pl.pallas_call(
            rows_kernel,
            out_shape=shape((1, ROWS, D), BF16),
            in_specs=[VMEM] * 5,
            out_specs=HBM,
            scratch_shapes=[
                pltpu.VMEM((24, D), BF16),
                pltpu.VMEM((BLOCK, D), F32),
                pltpu.VMEM((ROWS, D), BF16),
                pltpu.SemaphoreType.DMA((ROWS // BLOCK,)),
            ],
            compiler_params=PARAMS,
        )(grads, hidden, segment_ids, gain, upright)
    return loss, grad_rows


def solution(mesh):
    fine = Mesh(
        mesh.devices.reshape(N_X, N_Y, 2, N_ZH, N_ZL), ("x", "y", "core", "zh", "zl")
    )
    group, dp = ("x", "y", "core"), ("zh", "zl")
    placed = (P(group, dp, None), P(group, dp, None), P(group, dp), P(None, dp), P())
    return jax.shard_map(
        local,
        mesh=fine,
        in_specs=placed,
        out_specs=(P(group, dp), P(group, dp, None)),
        check_vma=False,
    )
```

```python
import functools

import jax
import jax.numpy as jnp
from jax import lax
from jax.experimental import pallas as pl
from jax.experimental.pallas import tpu as pltpu
from jax.sharding import Mesh
from jax.sharding import PartitionSpec as P

inv_tau = 20.0
loss_scale = 1024.0
norm_eps = 1e-06

F32 = jnp.float32
BF16 = jnp.bfloat16
ROWS = 256
D = 4096
HALF = D // 2
QUARTER = D // 4
PAS = 4
CHUNK = 2048
BLOCK = 64
META = 128
N_ZH = 3
N_ZL = 4
N_X = 4
N_Y = 8
BATCH = 256

VMEM = pl.BlockSpec(memory_space=pltpu.VMEM)
HBM = pl.BlockSpec(memory_space=pltpu.HBM)
PARAMS = pltpu.CompilerParams(vmem_limit_bytes=40 * 1024 * 1024)


def iota(shape, dim):
    return lax.broadcasted_iota(jnp.int32, shape, dim)


def split3(values):
    high = values.astype(BF16).astype(F32)
    rest = values - high
    middle = rest.astype(BF16).astype(F32)
    low = rest - middle
    return jnp.concatenate([high, middle, low], axis=0).astype(BF16)


def sum3(values):
    return values[0:8] + values[8:16] + values[16:24]


def pool_kernel(
    hidden_hbm, segment_hbm, assign_hbm, gain_hbm, positive_hbm,
    send_ref, upright_ref, partner_ref,
    hidden, segment_at, assign_at, gain, positive, chunk_sem, small_sem,
):
    chunks = [pl.ds(at * CHUNK, CHUNK) for at in range(D // CHUNK)]
    copies = [
        pltpu.make_async_copy(hidden_hbm.at[0, :, part], hidden.at[:, part], chunk_sem.at[at])
        for at, part in enumerate(chunks)
    ]
    small = [
        pltpu.make_async_copy(source, target, small_sem.at[at])
        for at, (source, target) in enumerate(
            [(segment_hbm, segment_at), (assign_hbm, assign_at), (positive_hbm, positive), (gain_hbm, gain)]
        )
    ]
    copies[0].start()
    for copy in small:
        copy.start()
    for copy in copies[1:]:
        copy.start()

    for copy in small:
        copy.wait()
    segment = jnp.broadcast_to(segment_at[0], (8, ROWS))
    onehot = jnp.where(segment == iota((8, ROWS), 0), 1.0, 0.0)
    counts = jnp.maximum(jnp.sum(onehot, axis=1, keepdims=True), 1.0)
    row = iota((8, META), 0)
    owner = jnp.zeros((8, META), jnp.int32)
    for k in range(PAS):
        owner = jnp.where(lax.rem(row, PAS) == k, assign_at[0:1, k : k + 1], owner)
    place = lax.axis_index("zl") * 16 + lax.axis_index("core") * 8 + row
    meta = jnp.where(iota((8, META), 1) == place, owner, 0).astype(F32).astype(BF16)
    for h in range(2):
        for peer in range(N_ZL):
            send_ref[peer, h, :, QUARTER:] = meta
    lane = iota((64, BATCH), 1)
    spread = jnp.where(lax.div(lane, PAS) == iota((64, BATCH), 0), 1.0, 0.0).astype(BF16)
    partner = jnp.concatenate([positive[...].astype(F32), jnp.zeros((PAS, 64), F32)], axis=0)
    partner = jnp.dot(partner.astype(BF16), spread, preferred_element_type=F32)
    partner = jnp.where(lax.rem(iota((8, BATCH), 1), PAS) == iota((8, BATCH), 0), partner, 0.0)
    partner_ref[...] = jnp.sum(partner, axis=0, keepdims=True).astype(jnp.int32)

    total = jnp.zeros((ROWS, 128), F32)
    for at, part in enumerate(chunks):
        copies[at].wait()
        for piece in range(0, CHUNK, 128):
            values = hidden[:, at * CHUNK + piece : at * CHUNK + piece + 128].astype(F32)
            total = total + values * values
    squares = jnp.sum(total.T, axis=0, keepdims=True)
    inverse = jnp.broadcast_to(lax.rsqrt(squares * (1.0 / D) + norm_eps), (8, ROWS))
    weights = split3(onehot * inverse)
    for h in range(2):
        columns = pl.ds(h * HALF, HALF)
        pooled = sum3(jnp.dot(weights, hidden[:, columns], preferred_element_type=F32))
        pooled = (pooled * gain[:, columns] / counts)[0:PAS]
        pooled = jnp.concatenate([pooled[:, 0:QUARTER], pooled[:, QUARTER:]], axis=0).astype(BF16)
        for peer in range(N_ZL):
            send_ref[peer, h, :, 0:QUARTER] = pooled
    upright_ref[...] = jnp.concatenate(
        [onehot, onehot, onehot, inverse, jnp.zeros((96, ROWS), F32)], axis=0
    ).T


def relay_kernel(pooled_ref, send_ref, back_ref):
    relay = lax.axis_index("zl")
    owners = jnp.sum(pooled_ref[:, QUARTER:].astype(F32), axis=0, keepdims=True)
    row = iota((128, META), 0)
    lane = iota((128, META), 1)
    slot = (lax.div(row, 8) * N_ZL + relay) * PAS + lax.rem(row, PAS)
    hit = (owners == slot.astype(F32)) & (lax.rem(lax.div(lane, 8), 2) == lax.div(lax.rem(row, 8), PAS))
    hit = hit & (row < N_ZH * 8) & (lane < 64)
    select = jnp.where(hit, 1.0, 0.0)
    back_ref[...] = select.T
    pooled = pooled_ref[:, 0:QUARTER]
    for q in range(2):
        part = jnp.where(lax.rem(lax.div(lane, PAS), 2) == q, select, 0.0)[0 : N_ZH * 8, 0:64]
        kept = jnp.dot(part.astype(BF16), pooled, preferred_element_type=F32)
        for peer in range(N_ZH):
            send_ref[peer, :, q * QUARTER : (q + 1) * QUARTER] = kept[
                peer * 8 : (peer + 1) * 8
            ].astype(BF16)


def owned_kernel(pooled_ref, send_ref, embed_ref):
    own = pooled_ref[0].astype(F32)
    for peer in range(1, N_ZH):
        own = own + pooled_ref[peer].astype(F32)
    embed_ref[...] = own
    send_ref[...] = own.astype(BF16)


def gram_kernel(embed_ref, gram_ref):
    embeds = embed_ref[...]
    gram_ref[...] = lax.dot_general(
        embeds, embeds, (((1,), (1,)), ((), ())), preferred_element_type=F32
    )


def contrast_kernel(gram_ref, batch_ref, embed_ref, partner_ref, loss_ref, send_ref):
    core = lax.axis_index("core")
    first = lax.axis_index("xh") * 2 + lax.axis_index("xl")
    first = ((first * 4 + lax.axis_index("yh")) * 2 + lax.axis_index("yl")) * 8
    shift = inv_tau
    row = iota((8, BATCH), 0)
    lane = iota((8, BATCH), 1)
    mine = first + row
    partner = partner_ref[...]
    own_partner = jnp.sum(jnp.where(lane == mine, partner, 0), axis=1, keepdims=True)

    gram = gram_ref[0] + gram_ref[1]
    everyone = iota((BATCH, BATCH), 0) == iota((BATCH, BATCH), 1)
    diagonal = jnp.where(everyone, gram, 0.0)
    across = lax.rsqrt(jnp.sum(diagonal, axis=0, keepdims=True) + norm_eps)
    down = lax.rsqrt(jnp.sum(diagonal, axis=1, keepdims=True) + norm_eps)
    logits = jnp.where(everyone, -1e30, gram * down * across * inv_tau)
    lse_all = shift + jnp.log(jnp.sum(jnp.exp(logits - shift), axis=0, keepdims=True))
    at = pl.ds(pl.multiple_of(first, 8), 8)
    own = gram_ref[0, at, :] + gram_ref[1, at, :]
    scale = lax.rsqrt(
        jnp.sum(jnp.where(lane == mine, own, 0.0), axis=1, keepdims=True) + norm_eps
    )
    cosine = own * scale * across
    own = jnp.where(lane == mine, -1e30, cosine * inv_tau)
    lse = shift + jnp.log(jnp.sum(jnp.exp(own - shift), axis=1, keepdims=True))
    hits = lane == own_partner
    loss = lse - jnp.sum(jnp.where(hits, own, 0.0), axis=1, keepdims=True)
    as_query = loss_scale * (jnp.exp(own - lse) - jnp.where(hits, 1.0, 0.0))
    as_key = loss_scale * (jnp.exp(own - lse_all) - jnp.where(partner == mine, 1.0, 0.0))
    weights = as_query.astype(BF16).astype(F32) + as_key.astype(BF16).astype(F32)
    inner = inv_tau * jnp.sum(weights * cosine, axis=1, keepdims=True)
    pair = jnp.concatenate([as_query, as_key], axis=0).astype(BF16)
    width = 512
    for start in range(0, HALF, width):
        columns = pl.ds(start, width)
        units = (batch_ref[:, columns].astype(F32) * down).astype(BF16)
        grad = jnp.dot(pair, units, preferred_element_type=F32)
        grad = (grad[0:8] + grad[8:16]) * inv_tau - embed_ref[:, columns] * (scale * inner)
        grad = (grad * scale).astype(BF16)
        for peer in range(N_ZH):
            send_ref[peer, :, columns] = grad
    place = (iota((8, 128), 1) + core * PAS) == iota((8, 128), 0)
    loss = jnp.sum(jnp.where(place, loss, 0.0), axis=0, keepdims=True)
    loss_ref[...] = loss[:, 0:PAS]


def back_kernel(grad_ref, back_ref, send_ref):
    back = back_ref[...]
    row = iota((128, META), 0)
    total = jnp.zeros((64, QUARTER), F32)
    for q in range(2):
        part = jnp.where(lax.rem(lax.div(row, PAS), 2) == q, back, 0.0)[0:64, 0 : N_ZH * 8]
        total = total + jnp.dot(
            part.astype(BF16),
            grad_ref[:, q * QUARTER : (q + 1) * QUARTER],
            preferred_element_type=F32,
        )
    total = total.astype(BF16)
    for peer in range(N_ZL):
        for c in range(2):
            at = (peer * 2 + c) * 8
            send_ref[peer, c] = total[at : at + 8]


def rows_kernel(
    grad_ref, hidden_ref, segment_ref, gain_ref, upright_ref, out_hbm,
    scaled, gained, out, sems,
):
    segment = jnp.broadcast_to(segment_ref[0], (8, ROWS))
    onehot = jnp.where(segment == iota((8, ROWS), 0), 1.0, 0.0)
    counts = jnp.maximum(jnp.sum(onehot, axis=1, keepdims=True), 1.0)
    for h in range(2):
        part = grad_ref[0, h].astype(F32)
        for peer in range(1, N_ZL):
            part = part + grad_ref[peer, h].astype(F32)
        for q in range(2):
            columns = pl.ds((h * 2 + q) * QUARTER, QUARTER)
            scaled[:, columns] = split3(gain_ref[:, columns] * (part / counts))
            part = jnp.concatenate([part[PAS:], part[0:PAS]], axis=0)
    width = 1024
    copies = []
    for start in range(0, ROWS, BLOCK):
        rows = pl.ds(start, BLOCK)
        spread = upright_ref[rows, 0:24].astype(BF16)
        inverse = upright_ref[rows, 24:25]
        total = jnp.zeros((BLOCK, 128), F32)
        for at in range(0, D, width):
            columns = pl.ds(at, width)
            part = jnp.dot(spread, scaled[:, columns], preferred_element_type=F32)
            gained[:, columns] = part
            part = part * hidden_ref[0, rows, columns].astype(F32)
            for piece in range(0, width, 128):
                total = total + part[:, piece : piece + 128]
        dot = jnp.sum(total, axis=1, keepdims=True) * (1.0 / D)
        cubed = inverse * inverse * inverse * dot
        for at in range(0, D, width):
            columns = pl.ds(at, width)
            values = hidden_ref[0, rows, columns].astype(F32)
            out[rows, columns] = (inverse * gained[:, columns] - values * cubed).astype(BF16)
        copy = pltpu.make_async_copy(out.at[rows], out_hbm.at[0, rows], sems.at[start // BLOCK])
        copy.start()
        copies.append(copy)
    for copy in copies:
        copy.wait()


def gather(block, axis, size):
    return lax.all_to_all(jnp.broadcast_to(block, (size,) + block.shape), axis, 0, 0)


Y_AXES, X_AXES = ("yl", "yh"), ("xh", "xl")


def along_y_x(block):
    column = gather(block, Y_AXES, N_Y).reshape(2, 4, 8, HALF).swapaxes(0, 1).reshape(N_Y * 8, HALF)
    return gather(column, X_AXES, N_X).reshape(BATCH, HALF)


def along_x_y(block):
    line = gather(block, X_AXES, N_X).reshape(N_X * 8, HALF)
    batch = gather(line, Y_AXES, N_Y)
    batch = batch.reshape((2, 4) + (N_X, 8, HALF)).transpose(2, 1, 0, 3, 4)
    return batch.reshape(BATCH, HALF)


def local(hidden, segment_ids, assign, positive, gain):
    shape = jax.ShapeDtypeStruct
    gain = gain.reshape(1, D)
    with jax.named_scope("pool"):
        send, upright, partner = pl.pallas_call(
            pool_kernel,
            out_shape=(
                shape((N_ZL, 2, 8, QUARTER + META), BF16),
                shape((ROWS, 128), F32),
                shape((1, BATCH), jnp.int32),
            ),
            in_specs=[HBM] * 5,
            out_specs=(VMEM, VMEM, VMEM),
            scratch_shapes=[
                pltpu.VMEM((ROWS, D), BF16),
                pltpu.VMEM((1, 1, ROWS), jnp.int32),
                pltpu.VMEM((1, PAS), jnp.int32),
                pltpu.VMEM((1, D), F32),
                pltpu.VMEM((PAS, 64), jnp.int32),
                pltpu.SemaphoreType.DMA((D // CHUNK,)),
                pltpu.SemaphoreType.DMA((4,)),
            ],
            compiler_params=PARAMS,
        )(*[pltpu.with_memory_space_constraint(v, pltpu.HBM) for v in (hidden, segment_ids, assign, gain, positive.T)])
    with jax.named_scope("pooled_to_relay"):
        send, core = lax.optimization_barrier((send, lax.axis_index("core")))
        pooled = lax.all_to_all(send.reshape(N_ZL * 2, 8, -1), ("zl", "core"), 0, 0)
        pooled = pooled.reshape(N_ZL * 2 * 8, -1)
    with jax.named_scope("relay"):
        send, back = pl.pallas_call(
            relay_kernel,
            out_shape=(shape((N_ZH, 8, HALF), BF16), shape((128, META), F32)),
            in_specs=[VMEM],
            out_specs=(VMEM, VMEM),
            compiler_params=PARAMS,
        )(pooled)
    with jax.named_scope("pooled_to_owner"):
        pooled = lax.all_to_all(send, "zh", 0, 0)
    with jax.named_scope("owned"):
        send, embed = pl.pallas_call(
            owned_kernel,
            out_shape=(shape((8, HALF), BF16), shape((8, HALF), F32)),
            in_specs=[VMEM],
            out_specs=(VMEM, VMEM),
            compiler_params=PARAMS,
        )(pooled)
    with jax.named_scope("embed_exchange"):
        send, core = lax.optimization_barrier((send, core))
        batch = lax.cond(core == 0, along_y_x, along_x_y, send)
    with jax.named_scope("gram"):
        gram = pl.pallas_call(
            gram_kernel,
            out_shape=shape((BATCH, BATCH), F32),
            in_specs=[VMEM],
            out_specs=VMEM,
            compiler_params=PARAMS,
        )(batch)
        gram = lax.all_gather(gram, "core", axis=0)
    with jax.named_scope("contrast"):
        loss, send = pl.pallas_call(
            contrast_kernel,
            out_shape=(shape((1, PAS), F32), shape((N_ZH, 8, HALF), BF16)),
            in_specs=[VMEM] * 4,
            out_specs=(VMEM, VMEM),
            compiler_params=PARAMS,
        )(gram, batch, embed, partner)
    with jax.named_scope("grad_to_relay"):
        grads = lax.all_to_all(send, "zh", 0, 0).reshape(N_ZH * 8, HALF)
    with jax.named_scope("back"):
        send = pl.pallas_call(
            back_kernel,
            out_shape=shape((N_ZL, 2, 8, QUARTER), BF16),
            in_specs=[VMEM, VMEM],
            out_specs=VMEM,
            compiler_params=PARAMS,
        )(grads, back)
    with jax.named_scope("grad_to_rows"):
        grads = lax.all_to_all(send.reshape(N_ZL * 2, 8, QUARTER), ("zl", "core"), 0, 0)
        grads = grads.reshape(N_ZL, 2, 8, QUARTER)
    with jax.named_scope("rows"):
        grad_rows = pl.pallas_call(
            rows_kernel,
            out_shape=shape((1, ROWS, D), BF16),
            in_specs=[VMEM] * 5,
            out_specs=HBM,
            scratch_shapes=[
                pltpu.VMEM((24, D), BF16),
                pltpu.VMEM((BLOCK, D), F32),
                pltpu.VMEM((ROWS, D), BF16),
                pltpu.SemaphoreType.DMA((ROWS // BLOCK,)),
            ],
            compiler_params=PARAMS,
        )(grads, hidden, segment_ids, gain, upright)
    return loss, grad_rows


def solution(mesh):
    fine = Mesh(
        mesh.devices.reshape(2, 2, 4, 2, 2, N_ZH, N_ZL),
        ("xh", "xl", "yh", "yl", "core", "zh", "zl"),
    )
    group, dp = ("xh", "xl", "yh", "yl", "core"), ("zh", "zl")
    placed = (P(group, dp, None), P(group, dp, None), P(group, dp), P(None, dp), P())
    return jax.shard_map(
        local,
        mesh=fine,
        in_specs=placed,
        out_specs=(P(group, dp), P(group, dp, None)),
        check_vma=False,
    )
```

```python
import functools

import jax
import jax.numpy as jnp
from jax import lax
from jax.experimental import pallas as pl
from jax.experimental.pallas import tpu as pltpu
from jax.sharding import Mesh
from jax.sharding import PartitionSpec as P

inv_tau = 20.0
loss_scale = 1024.0
norm_eps = 1e-06

F32 = jnp.float32
BF16 = jnp.bfloat16
ROWS = 256
D = 4096
HALF = D // 2
QUARTER = D // 4
PAS = 4
CHUNK = 2048
BLOCK = 64
META = 128
N_ZH = 3
N_ZL = 4
N_X = 4
N_Y = 8
BATCH = 256

VMEM = pl.BlockSpec(memory_space=pltpu.VMEM)
HBM = pl.BlockSpec(memory_space=pltpu.HBM)
PARAMS = pltpu.CompilerParams(vmem_limit_bytes=40 * 1024 * 1024)


def iota(shape, dim):
    return lax.broadcasted_iota(jnp.int32, shape, dim)


def split3(values):
    high = values.astype(BF16).astype(F32)
    rest = values - high
    middle = rest.astype(BF16).astype(F32)
    low = rest - middle
    return jnp.concatenate([high, middle, low], axis=0).astype(BF16)


def sum3(values):
    return values[0:8] + values[8:16] + values[16:24]


def pool_kernel(
    hidden_hbm, segment_hbm, assign_hbm, gain_hbm, positive_hbm,
    send_ref, upright_ref, partner_ref,
    hidden, segment_at, assign_at, gain, positive, chunk_sem, small_sem,
):
    chunks = [pl.ds(at * CHUNK, CHUNK) for at in range(D // CHUNK)]
    copies = [
        pltpu.make_async_copy(hidden_hbm.at[0, :, part], hidden.at[:, part], chunk_sem.at[at])
        for at, part in enumerate(chunks)
    ]
    small = [
        pltpu.make_async_copy(source, target, small_sem.at[at])
        for at, (source, target) in enumerate(
            [(segment_hbm, segment_at), (assign_hbm, assign_at), (positive_hbm, positive), (gain_hbm, gain)]
        )
    ]
    copies[0].start()
    for copy in small:
        copy.start()
    for copy in copies[1:]:
        copy.start()

    for copy in small:
        copy.wait()
    segment = jnp.broadcast_to(segment_at[0], (8, ROWS))
    onehot = jnp.where(segment == iota((8, ROWS), 0), 1.0, 0.0)
    counts = jnp.maximum(jnp.sum(onehot, axis=1, keepdims=True), 1.0)
    row = iota((8, META), 0)
    owner = jnp.zeros((8, META), jnp.int32)
    for k in range(PAS):
        owner = jnp.where(lax.rem(row, PAS) == k, assign_at[0:1, k : k + 1], owner)
    place = (lax.axis_index("zb") * 2 + lax.axis_index("za")) * 16
    place = place + lax.axis_index("core") * 8 + row
    meta = jnp.where(iota((8, META), 1) == place, owner, 0).astype(F32).astype(BF16)
    for h in range(2):
        for peer in range(N_ZL):
            send_ref[peer, h, :, QUARTER:] = meta
    lane = iota((64, BATCH), 1)
    spread = jnp.where(lax.div(lane, PAS) == iota((64, BATCH), 0), 1.0, 0.0).astype(BF16)
    partner = jnp.concatenate([positive[...].astype(F32), jnp.zeros((PAS, 64), F32)], axis=0)
    partner = jnp.dot(partner.astype(BF16), spread, preferred_element_type=F32)
    partner = jnp.where(lax.rem(iota((8, BATCH), 1), PAS) == iota((8, BATCH), 0), partner, 0.0)
    partner_ref[...] = jnp.sum(partner, axis=0, keepdims=True).astype(jnp.int32)

    total = jnp.zeros((ROWS, 128), F32)
    for at, part in enumerate(chunks):
        copies[at].wait()
        for piece in range(0, CHUNK, 128):
            values = hidden[:, at * CHUNK + piece : at * CHUNK + piece + 128].astype(F32)
            total = total + values * values
    squares = jnp.sum(total.T, axis=0, keepdims=True)
    inverse = jnp.broadcast_to(lax.rsqrt(squares * (1.0 / D) + norm_eps), (8, ROWS))
    weights = split3(onehot * inverse)
    for h in range(2):
        columns = pl.ds(h * HALF, HALF)
        pooled = sum3(jnp.dot(weights, hidden[:, columns], preferred_element_type=F32))
        pooled = (pooled * gain[:, columns] / counts)[0:PAS]
        pooled = jnp.concatenate([pooled[:, 0:QUARTER], pooled[:, QUARTER:]], axis=0).astype(BF16)
        for peer in range(N_ZL):
            send_ref[peer, h, :, 0:QUARTER] = pooled
    upright_ref[...] = jnp.concatenate(
        [onehot, onehot, onehot, inverse, jnp.zeros((96, ROWS), F32)], axis=0
    ).T


def relay_kernel(pooled_ref, send_ref, back_ref):
    relay = lax.axis_index("za") * 2 + lax.axis_index("zb")
    owners = jnp.sum(pooled_ref[:, QUARTER:].astype(F32), axis=0, keepdims=True)
    row = iota((128, META), 0)
    lane = iota((128, META), 1)
    slot = (lax.div(row, 8) * N_ZL + relay) * PAS + lax.rem(row, PAS)
    hit = (owners == slot.astype(F32)) & (lax.rem(lax.div(lane, 8), 2) == lax.div(lax.rem(row, 8), PAS))
    hit = hit & (row < N_ZH * 8) & (lane < 64)
    select = jnp.where(hit, 1.0, 0.0)
    back_ref[...] = select.T
    pooled = pooled_ref[:, 0:QUARTER]
    for q in range(2):
        part = jnp.where(lax.rem(lax.div(lane, PAS), 2) == q, select, 0.0)[0 : N_ZH * 8, 0:64]
        kept = jnp.dot(part.astype(BF16), pooled, preferred_element_type=F32)
        for peer in range(N_ZH):
            send_ref[peer, :, q * QUARTER : (q + 1) * QUARTER] = kept[
                peer * 8 : (peer + 1) * 8
            ].astype(BF16)


def owned_kernel(pooled_ref, send_ref, embed_ref):
    own = pooled_ref[0].astype(F32)
    for peer in range(1, N_ZH):
        own = own + pooled_ref[peer].astype(F32)
    embed_ref[...] = own
    send_ref[...] = own.astype(BF16)


def gram_kernel(embed_ref, gram_ref):
    embeds = embed_ref[...]
    gram_ref[...] = lax.dot_general(
        embeds, embeds, (((1,), (1,)), ((), ())), preferred_element_type=F32
    )


def contrast_kernel(gram_ref, batch_ref, embed_ref, partner_ref, loss_ref, send_ref):
    core = lax.axis_index("core")
    first = lax.axis_index("xh") * 2 + lax.axis_index("xl")
    first = ((first * 4 + lax.axis_index("yh")) * 2 + lax.axis_index("yl")) * 8
    shift = inv_tau
    row = iota((8, BATCH), 0)
    lane = iota((8, BATCH), 1)
    mine = first + row
    partner = partner_ref[...]
    own_partner = jnp.sum(jnp.where(lane == mine, partner, 0), axis=1, keepdims=True)

    gram = gram_ref[0] + gram_ref[1]
    everyone = iota((BATCH, BATCH), 0) == iota((BATCH, BATCH), 1)
    diagonal = jnp.where(everyone, gram, 0.0)
    across = lax.rsqrt(jnp.sum(diagonal, axis=0, keepdims=True) + norm_eps)
    down = lax.rsqrt(jnp.sum(diagonal, axis=1, keepdims=True) + norm_eps)
    logits = jnp.where(everyone, -1e30, gram * down * across * inv_tau)
    lse_all = shift + jnp.log(jnp.sum(jnp.exp(logits - shift), axis=0, keepdims=True))
    at = pl.ds(pl.multiple_of(first, 8), 8)
    own = gram_ref[0, at, :] + gram_ref[1, at, :]
    scale = lax.rsqrt(
        jnp.sum(jnp.where(lane == mine, own, 0.0), axis=1, keepdims=True) + norm_eps
    )
    cosine = own * scale * across
    own = jnp.where(lane == mine, -1e30, cosine * inv_tau)
    lse = shift + jnp.log(jnp.sum(jnp.exp(own - shift), axis=1, keepdims=True))
    hits = lane == own_partner
    loss = lse - jnp.sum(jnp.where(hits, own, 0.0), axis=1, keepdims=True)
    as_query = loss_scale * (jnp.exp(own - lse) - jnp.where(hits, 1.0, 0.0))
    as_key = loss_scale * (jnp.exp(own - lse_all) - jnp.where(partner == mine, 1.0, 0.0))
    weights = as_query.astype(BF16).astype(F32) + as_key.astype(BF16).astype(F32)
    inner = inv_tau * jnp.sum(weights * cosine, axis=1, keepdims=True)
    pair = jnp.concatenate([as_query, as_key], axis=0).astype(BF16)
    width = 512
    for start in range(0, HALF, width):
        columns = pl.ds(start, width)
        units = (batch_ref[:, columns].astype(F32) * down).astype(BF16)
        grad = jnp.dot(pair, units, preferred_element_type=F32)
        grad = (grad[0:8] + grad[8:16]) * inv_tau - embed_ref[:, columns] * (scale * inner)
        grad = (grad * scale).astype(BF16)
        for peer in range(N_ZH):
            send_ref[peer, :, columns] = grad
    place = (iota((8, 128), 1) + core * PAS) == iota((8, 128), 0)
    loss = jnp.sum(jnp.where(place, loss, 0.0), axis=0, keepdims=True)
    loss_ref[...] = loss[:, 0:PAS]


def back_kernel(grad_ref, back_ref, send_ref):
    back = back_ref[...]
    row = iota((128, META), 0)
    total = jnp.zeros((64, QUARTER), F32)
    for q in range(2):
        part = jnp.where(lax.rem(lax.div(row, PAS), 2) == q, back, 0.0)[0:64, 0 : N_ZH * 8]
        total = total + jnp.dot(
            part.astype(BF16),
            grad_ref[:, q * QUARTER : (q + 1) * QUARTER],
            preferred_element_type=F32,
        )
    total = total.astype(BF16)
    for peer in range(N_ZL):
        for c in range(2):
            at = (peer * 2 + c) * 8
            send_ref[peer, c] = total[at : at + 8]


def rows_kernel(
    grad_ref, hidden_ref, segment_ref, gain_ref, upright_ref, out_hbm,
    scaled, gained, out, sems,
):
    segment = jnp.broadcast_to(segment_ref[0], (8, ROWS))
    onehot = jnp.where(segment == iota((8, ROWS), 0), 1.0, 0.0)
    counts = jnp.maximum(jnp.sum(onehot, axis=1, keepdims=True), 1.0)
    for h in range(2):
        part = grad_ref[0, h].astype(F32)
        for peer in range(1, N_ZL):
            part = part + grad_ref[peer, h].astype(F32)
        for q in range(2):
            columns = pl.ds((h * 2 + q) * QUARTER, QUARTER)
            scaled[:, columns] = split3(gain_ref[:, columns] * (part / counts))
            part = jnp.concatenate([part[PAS:], part[0:PAS]], axis=0)
    width = 1024
    copies = []
    for start in range(0, ROWS, BLOCK):
        rows = pl.ds(start, BLOCK)
        spread = upright_ref[rows, 0:24].astype(BF16)
        inverse = upright_ref[rows, 24:25]
        total = jnp.zeros((BLOCK, 128), F32)
        for at in range(0, D, width):
            columns = pl.ds(at, width)
            part = jnp.dot(spread, scaled[:, columns], preferred_element_type=F32)
            gained[:, columns] = part
            part = part * hidden_ref[0, rows, columns].astype(F32)
            for piece in range(0, width, 128):
                total = total + part[:, piece : piece + 128]
        dot = jnp.sum(total, axis=1, keepdims=True) * (1.0 / D)
        cubed = inverse * inverse * inverse * dot
        for at in range(0, D, width):
            columns = pl.ds(at, width)
            values = hidden_ref[0, rows, columns].astype(F32)
            out[rows, columns] = (inverse * gained[:, columns] - values * cubed).astype(BF16)
        copy = pltpu.make_async_copy(out.at[rows], out_hbm.at[0, rows], sems.at[start // BLOCK])
        copy.start()
        copies.append(copy)
    for copy in copies:
        copy.wait()


def gather(block, axis, size):
    return lax.all_to_all(jnp.broadcast_to(block, (size,) + block.shape), axis, 0, 0)


Y_AXES, X_AXES = ("yl", "yh"), ("xh", "xl")


def along_y_x(block):
    column = gather(block, Y_AXES, N_Y).reshape(2, 4, 8, HALF).swapaxes(0, 1).reshape(N_Y * 8, HALF)
    return gather(column, X_AXES, N_X).reshape(BATCH, HALF)


def along_x_y(block):
    line = gather(block, X_AXES, N_X).reshape(N_X * 8, HALF)
    batch = gather(line, Y_AXES, N_Y)
    batch = batch.reshape((2, 4) + (N_X, 8, HALF)).transpose(2, 1, 0, 3, 4)
    return batch.reshape(BATCH, HALF)


def local(hidden, segment_ids, assign, positive, gain):
    shape = jax.ShapeDtypeStruct
    gain = gain.reshape(1, D)
    with jax.named_scope("pool"):
        send, upright, partner = pl.pallas_call(
            pool_kernel,
            out_shape=(
                shape((N_ZL, 2, 8, QUARTER + META), BF16),
                shape((ROWS, 128), F32),
                shape((1, BATCH), jnp.int32),
            ),
            in_specs=[HBM] * 5,
            out_specs=(VMEM, VMEM, VMEM),
            scratch_shapes=[
                pltpu.VMEM((ROWS, D), BF16),
                pltpu.VMEM((1, 1, ROWS), jnp.int32),
                pltpu.VMEM((1, PAS), jnp.int32),
                pltpu.VMEM((1, D), F32),
                pltpu.VMEM((PAS, 64), jnp.int32),
                pltpu.SemaphoreType.DMA((D // CHUNK,)),
                pltpu.SemaphoreType.DMA((4,)),
            ],
            compiler_params=PARAMS,
        )(*[pltpu.with_memory_space_constraint(v, pltpu.HBM) for v in (hidden, segment_ids, assign, gain, positive.T)])
    with jax.named_scope("pooled_to_relay"):
        send, core = lax.optimization_barrier((send, lax.axis_index("core")))
        pooled = lax.all_to_all(send.reshape(N_ZL * 2, 8, -1), ("zb", "za", "core"), 0, 0)
        pooled = pooled.reshape(N_ZL * 2 * 8, -1)
    with jax.named_scope("relay"):
        send, back = pl.pallas_call(
            relay_kernel,
            out_shape=(shape((N_ZH, 8, HALF), BF16), shape((128, META), F32)),
            in_specs=[VMEM],
            out_specs=(VMEM, VMEM),
            compiler_params=PARAMS,
        )(pooled)
    with jax.named_scope("pooled_to_owner"):
        pooled = lax.all_to_all(send, "zh", 0, 0)
    with jax.named_scope("owned"):
        send, embed = pl.pallas_call(
            owned_kernel,
            out_shape=(shape((8, HALF), BF16), shape((8, HALF), F32)),
            in_specs=[VMEM],
            out_specs=(VMEM, VMEM),
            compiler_params=PARAMS,
        )(pooled)
    with jax.named_scope("embed_exchange"):
        send, core = lax.optimization_barrier((send, core))
        batch = lax.cond(core == 0, along_y_x, along_x_y, send)
    with jax.named_scope("gram"):
        gram = pl.pallas_call(
            gram_kernel,
            out_shape=shape((BATCH, BATCH), F32),
            in_specs=[VMEM],
            out_specs=VMEM,
            compiler_params=PARAMS,
        )(batch)
        gram = lax.all_gather(gram, "core", axis=0)
    with jax.named_scope("contrast"):
        loss, send = pl.pallas_call(
            contrast_kernel,
            out_shape=(shape((1, PAS), F32), shape((N_ZH, 8, HALF), BF16)),
            in_specs=[VMEM] * 4,
            out_specs=(VMEM, VMEM),
            compiler_params=PARAMS,
        )(gram, batch, embed, partner)
    with jax.named_scope("grad_to_relay"):
        grads = lax.all_to_all(send, "zh", 0, 0).reshape(N_ZH * 8, HALF)
    with jax.named_scope("back"):
        send = pl.pallas_call(
            back_kernel,
            out_shape=shape((N_ZL, 2, 8, QUARTER), BF16),
            in_specs=[VMEM, VMEM],
            out_specs=VMEM,
            compiler_params=PARAMS,
        )(grads, back)
    with jax.named_scope("grad_to_rows"):
        grads = lax.all_to_all(send.reshape(N_ZL * 2, 8, QUARTER), ("zb", "za", "core"), 0, 0)
        grads = grads.reshape(N_ZL, 2, 8, QUARTER)
    with jax.named_scope("rows"):
        grad_rows = pl.pallas_call(
            rows_kernel,
            out_shape=shape((1, ROWS, D), BF16),
            in_specs=[VMEM] * 5,
            out_specs=HBM,
            scratch_shapes=[
                pltpu.VMEM((24, D), BF16),
                pltpu.VMEM((BLOCK, D), F32),
                pltpu.VMEM((ROWS, D), BF16),
                pltpu.SemaphoreType.DMA((ROWS // BLOCK,)),
            ],
            compiler_params=PARAMS,
        )(grads, hidden, segment_ids, gain, upright)
    return loss, grad_rows


def solution(mesh):
    fine = Mesh(
        mesh.devices.reshape(2, 2, 4, 2, 2, N_ZH, 2, 2),
        ("xh", "xl", "yh", "yl", "core", "zh", "za", "zb"),
    )
    group, dp = ("xh", "xl", "yh", "yl", "core"), ("zh", "za", "zb")
    placed = (P(group, dp, None), P(group, dp, None), P(group, dp), P(None, dp), P())
    return jax.shard_map(
        local,
        mesh=fine,
        in_specs=placed,
        out_specs=(P(group, dp), P(group, dp, None)),
        check_vma=False,
    )
```
